512 devices in a mesh: blk: 4 (over x), dp: 128 (over z, y, core).
Axes of the slice: x: 4, y: 8, z: 8, core: 2. Of those that a mesh axis runs over, the one named last changes fastest.
Arguments:
- q_raw: bfloat16 [65536, 2048], P(('dp', 'blk')), may hold values from -6 to 6
- k_raw: bfloat16 [65536, 2048], P(('dp', 'blk')), may hold values from -6 to 6
- values: bfloat16 [65536, 2048], P(('dp', 'blk')), may hold values from -6 to 6
- grad_out: bfloat16 [65536, 2048], P(('dp', 'blk')), may hold values from -6 to 6
- q_gain: float32 [2048], replicated, may hold values from 0.5 to 5.5
- k_gain: float32 [2048], replicated, may hold values from 0.5 to 5.5
- patch_counts: int32 [512], replicated, may hold values from 0 to 512, as said below
- assignment: int32 [512], replicated, may hold values from 0 to 127, as said below
- loader_shard: int32 [512], replicated, may hold values from 0 to 127
Outputs:
- attended: bfloat16 [65536, 2048], P(('dp', 'blk'))
- q_grad: bfloat16 [65536, 2048], P(('dp', 'blk'))
- k_grad: bfloat16 [65536, 2048], P(('dp', 'blk'))
- v_grad: bfloat16 [65536, 2048], P(('dp', 'blk'))
- q_gain_grad: float32 [2048], replicated
- k_gain_grad: float32 [2048], replicated
The draws below stay inside these ranges and needn't reach their ends.
Inputs may be any that keep to these rules, and one draw needn't show every extreme that they name: `patch_counts`: an entry of 0 is no image; every other count is 128 or more; the counts of the entries assigned to one group sum to 512; each group has 1 to half of 4 images; some image fills a whole group. `assignment`: every group is named by some entry with a positive count.
All inputs are finite; a program needn't handle non-finite values.
Results may differ from the reference program's by a relative error of at most 0.04.
The reference program's roundings to bfloat16 on the way (of `grad_weighted` and `softmax_half`) count: a program that leaves them out, or rounds other values in their place, can miss the bound.
Values may be sent and summed in bfloat16 or wider, within the bound.
No kernel may reach another device: no remote copies, remote signals or barrier semaphores. Data moves between devices by JAX's collectives and lax.ppermute only.
A program may use at most 64 MiB of HBM per device.

```python
import math
import jax
import jax.numpy as jnp
from jax import lax

HEADS = 16
HEAD_DIM = 128
TOK_DEV = 128
CYCLE = 4
GROUPS = 128
WIDTH = 2048
SLOTS = 512
IMAGES = 512
TOKENS = 65536


def image_table(key):
    number = jax.random.randint(jax.random.fold_in(key, 21), (GROUPS,), 1, CYCLE // 2 + 1)
    single = jax.random.randint(jax.random.fold_in(key, 22), (), 0, GROUPS)
    number = jnp.where(jnp.arange(GROUPS) == single, 1, number)
    spare = SLOTS - number * TOK_DEV
    cuts = jax.random.randint(jax.random.fold_in(key, 23), (GROUPS, CYCLE - 1), 0, spare[:, None] + 1)
    cuts = jnp.sort(cuts, axis=1)
    column = jnp.arange(CYCLE - 1)[None, :]
    cuts = jnp.where(column >= number[:, None] - 1, spare[:, None], cuts)
    bounds = jnp.concatenate([jnp.zeros((GROUPS, 1), jnp.int32), cuts, spare[:, None]], axis=1)
    widths_each = bounds[:, 1:] - bounds[:, :-1]
    position = jnp.arange(CYCLE)[None, :]
    counts = jnp.where(position < number[:, None], TOK_DEV + widths_each, 0)
    owners = jnp.broadcast_to(jnp.arange(GROUPS)[:, None], (GROUPS, CYCLE))
    order = jax.random.permutation(jax.random.fold_in(key, 24), IMAGES)
    return (counts.reshape(IMAGES)[order].astype(jnp.int32), owners.reshape(IMAGES)[order].astype(jnp.int32))


def raw_bases(key):
    query_base = jax.random.normal(jax.random.fold_in(key, 31), (TOKENS, WIDTH), jnp.float32)
    key_base = jax.random.normal(jax.random.fold_in(key, 32), (TOKENS, WIDTH), jnp.float32)
    return (query_base, key_base)


def draw_patch_counts(key, part):
    counts, owners = image_table(key)
    return counts


def draw_assignment(key, part):
    counts, owners = image_table(key)
    return owners


def draw_q_raw(key, part):
    query_base, key_base = raw_bases(key)
    return jnp.clip(query_base, -6.0, 6.0).astype(jnp.bfloat16)


def draw_k_raw(key, part):
    query_base, key_base = raw_bases(key)
    return jnp.clip(key_base, -6.0, 6.0).astype(jnp.bfloat16)


def draw_q_gain(key, part):
    key = jax.random.fold_in(key, 4)
    return jnp.exp(jax.random.uniform(key, (WIDTH,), jnp.float32, math.log(0.5), math.log(2.0)))


def draw_k_gain(key, part):
    key = jax.random.fold_in(key, 5)
    return jnp.exp(jax.random.uniform(key, (WIDTH,), jnp.float32, math.log(0.5), math.log(2.0)))


def place_ends(values, stream_key, smallest, largest):
    dims = values.shape
    place = [jax.random.randint(jax.random.fold_in(stream_key, axis), (), 0, dims[axis]) for axis in range(len(dims))]
    values = values.at[tuple(place)].set(smallest)
    longest = dims.index(max(dims))
    place[longest] = (place[longest] + 1) % dims[longest]
    return values.at[tuple(place)].set(largest)


def steps_of(own_key, shape, cuts, low, high):
    loudness = 1.0
    for axis_at, parts in cuts:
        draws = jax.random.uniform(jax.random.fold_in(jax.random.fold_in(own_key, 6), axis_at), (parts,), jnp.float32, low / len(cuts), high / len(cuts))
        loudness = loudness * jnp.repeat(jnp.exp(draws), shape[axis_at] // parts).reshape((-1,) + (1,) * (len(shape) - 1 - axis_at))
    return loudness


def normal_values(rng, extent, scale, limit, shards=(), held_as=jnp.bfloat16):
    drawn = jax.random.normal(rng, extent, jnp.float32) * scale
    if len(shards) > 0:
        drawn = steps_of(rng, extent, shards, -0.22, 0.18) * drawn
    return jnp.clip(drawn, min=-limit, max=limit).astype(held_as)


def setup_inputs(seed: int = 0) -> dict:
    arg_keys = jax.random.split(jax.random.key(seed), 10)
    q_raw = draw_q_raw(jax.random.fold_in(arg_keys[9], 71), 0)
    k_raw = draw_k_raw(jax.random.fold_in(arg_keys[9], 71), 0)
    values = normal_values(arg_keys[2], (TOKENS, WIDTH), 1.0, 6.0, ((0, 512),))
    grad_out = normal_values(arg_keys[3], (TOKENS, WIDTH), 1.0, 6.0, ((0, 512),))
    q_gain = draw_q_gain(jax.random.fold_in(arg_keys[9], 71), 0)
    k_gain = draw_k_gain(jax.random.fold_in(arg_keys[9], 71), 0)
    patch_counts = draw_patch_counts(jax.random.fold_in(arg_keys[9], 71), 0)
    assignment = draw_assignment(jax.random.fold_in(arg_keys[9], 71), 0)
    loader_shard = place_ends(jax.random.randint(arg_keys[8], (IMAGES,), 0, GROUPS), jax.random.fold_in(arg_keys[8], 1), 0, GROUPS - 1).astype(jnp.int32)
    return {"q_raw": q_raw, "k_raw": k_raw, "values": values, "grad_out": grad_out, "q_gain": q_gain, "k_gain": k_gain, "patch_counts": patch_counts, "assignment": assignment, "loader_shard": loader_shard}


epsilon = 1e-06
masked_score = -1e+30

def image_weights(patch_counts, loader_shard):
    living = patch_counts > 0
    shared = (loader_shard[:, None] == loader_shard[None, :]) & living[None, :]
    per_loader = lax.optimization_barrier(jnp.sum(shared.astype(jnp.int32), axis=1)).astype(jnp.int32)
    per_loader = jnp.where(living, per_loader, 1)
    living_total = jnp.sum(living.astype(jnp.int32)).astype(jnp.int32)
    return living_total.astype(jnp.float32) / (GROUPS * per_loader).astype(jnp.float32)

def row_layout(patch_counts, assignment, image_weight, group_index, first_row, row_total):
    owned = jnp.where(assignment == group_index, patch_counts, 0)
    offsets = (jnp.cumsum(owned) - owned).astype(jnp.int32)
    positions = first_row + jnp.arange(row_total, dtype=jnp.int32)
    inside = (positions[:, None] >= offsets[None, :]) & (positions[:, None] < (offsets + owned)[None, :])
    entries = jnp.arange(patch_counts.shape[0], dtype=jnp.int32)
    segments = lax.optimization_barrier(jnp.sum(jnp.where(inside, entries[None, :], 0), axis=1)).astype(jnp.int32)
    row_weight = lax.optimization_barrier(jnp.sum(jnp.where(inside, image_weight[None, :], 0.0), axis=1))
    return (segments, row_weight)

def normed(raw, gain):
    widened = raw.astype(jnp.float32)
    inverse = lax.rsqrt(lax.optimization_barrier(jnp.mean(widened * widened, axis=-1, keepdims=True)) + epsilon)
    unit_rows = widened * inverse
    return (unit_rows, inverse, (unit_rows * gain).astype(jnp.bfloat16))

def norm_back(grad_normed, unit_rows, inverse, gain):
    grad_unit = grad_normed * gain
    grad_raw = inverse * (grad_unit - unit_rows * lax.optimization_barrier(jnp.mean(grad_unit * unit_rows, axis=-1, keepdims=True)))
    return (grad_raw.astype(jnp.bfloat16), lax.optimization_barrier(jnp.sum(grad_normed * unit_rows, axis=0)))

def head_pass(query_head, key_head, value_head, grad_head, same_image):
    score_scale = HEAD_DIM ** (-0.5)
    scores = jnp.dot(query_head, key_head.T, preferred_element_type=jnp.float32) * score_scale
    scores = jnp.where(same_image, scores, masked_score)
    row_max = lax.optimization_barrier(jnp.max(scores, axis=1, keepdims=True))
    log_total = row_max + jnp.log(lax.optimization_barrier(jnp.sum(jnp.exp(scores - row_max), axis=1, keepdims=True)))
    softmax = jnp.where(same_image, jnp.exp(scores - log_total), 0.0)
    softmax_half = softmax.astype(jnp.bfloat16)
    attended_full = jnp.dot(softmax_half, value_head, preferred_element_type=jnp.float32)
    grad_scores = jnp.dot(grad_head, value_head.T, preferred_element_type=jnp.float32)
    row_delta = lax.optimization_barrier(jnp.sum(grad_head.astype(jnp.float32) * attended_full, axis=1, keepdims=True))
    weighted_half = (softmax * grad_scores).astype(jnp.bfloat16)
    query_grad = score_scale * (jnp.dot(weighted_half, key_head, preferred_element_type=jnp.float32) - row_delta * jnp.dot(softmax_half, key_head, preferred_element_type=jnp.float32))
    score_grad_half = (softmax * (grad_scores - row_delta)).astype(jnp.bfloat16)
    key_grad = score_scale * jnp.dot(score_grad_half.T, query_head, preferred_element_type=jnp.float32)
    value_grad = jnp.dot(softmax_half.T, grad_head, preferred_element_type=jnp.float32)
    return (attended_full, query_grad, key_grad, value_grad)

def split_heads(array):
    return array.reshape(SLOTS, HEADS, HEAD_DIM).transpose(1, 0, 2)

def merge_heads(array):
    return array.transpose(1, 0, 2).reshape(SLOTS, WIDTH)

def group_pass(group_index, q_rows, k_rows, value_rows, grad_rows, q_gain, k_gain, patch_counts, assignment, image_weight):
    segments, row_weight = row_layout(patch_counts, assignment, image_weight, group_index, jnp.int32(0), SLOTS)
    query_unit, query_inverse, query_normed = normed(q_rows, q_gain)
    key_unit, key_inverse, key_normed = normed(k_rows, k_gain)
    grad_weighted = (grad_rows.astype(jnp.float32) * row_weight[:, None]).astype(jnp.bfloat16)
    same_image = segments[:, None] == segments[None, :]

    def one_head(bundle):
        return head_pass(bundle[0], bundle[1], bundle[2], bundle[3], same_image)
    results = lax.map(one_head, (split_heads(query_normed), split_heads(key_normed), split_heads(value_rows), split_heads(grad_weighted)))
    attended_full, query_grad, key_grad, value_grad = [merge_heads(item) for item in results]
    q_grad, q_part = norm_back(query_grad, query_unit, query_inverse, q_gain)
    k_grad, k_part = norm_back(key_grad, key_unit, key_inverse, k_gain)
    return (attended_full.astype(jnp.bfloat16), q_grad, k_grad, value_grad.astype(jnp.bfloat16), q_part, k_part)

def reference(q_raw, k_raw, values, grad_out, q_gain, k_gain, patch_counts, assignment, loader_shard):
    image_weight = image_weights(patch_counts, loader_shard)

    def grouped(array):
        return array.reshape(GROUPS, SLOTS, WIDTH)

    def one_group(bundle):
        return group_pass(bundle[0], bundle[1], bundle[2], bundle[3], bundle[4], q_gain, k_gain, patch_counts, assignment, image_weight)
    results = lax.map(one_group, (jnp.arange(GROUPS, dtype=jnp.int32), grouped(q_raw), grouped(k_raw), grouped(values), grouped(grad_out)))
    attended, q_grad, k_grad, v_grad, q_parts, k_parts = results

    def flat(array):
        return array.reshape(TOKENS, WIDTH)
    return (flat(attended), flat(q_grad), flat(k_grad), flat(v_grad), lax.optimization_barrier(jnp.sum(q_parts, axis=0)), lax.optimization_barrier(jnp.sum(k_parts, axis=0)))
```

```python
import functools

import jax
import jax.numpy as jnp
from jax import lax
from jax.experimental import pallas as pl
from jax.experimental.pallas import tpu as pltpu
from jax.sharding import Mesh, PartitionSpec as P

HEAD_DIM = 128
ROW_STEP = 32

epsilon = 1e-06
masked_score = -1e30
log2_e = 1.4426950408889634


def unit_of(raw):
    widened = raw.astype(jnp.float32)
    inverse = lax.rsqrt(jnp.mean(widened * widened, axis=-1, keepdims=True) + epsilon)
    return widened * inverse, inverse


def group_table(counts, assignment, loader, group_index, group_count):
    shape = counts.shape
    entries = lax.broadcasted_iota(jnp.int32, shape, 0) * shape[1] + lax.broadcasted_iota(
        jnp.int32, shape, 1
    )
    living = counts > 0
    owned = living & (assignment == group_index)
    total = shape[0] * shape[1]
    first = jnp.min(jnp.where(owned, entries, total))
    last = jnp.max(jnp.where(owned, entries, -1))
    boundary = jnp.sum(jnp.where(entries == first, counts, 0))
    living_total = jnp.sum(living.astype(jnp.int32))

    def weight_of(entry):
        shard = jnp.sum(jnp.where(entries == entry, loader, 0))
        shared = jnp.sum((living & (loader == shard)).astype(jnp.int32))
        shared = jnp.full((1, 1), group_count * shared, jnp.int32)
        return jnp.full((1, 1), living_total, jnp.int32).astype(jnp.float32) / shared.astype(jnp.float32)

    return boundary, weight_of(first), weight_of(last)


def pack_kernel(
    group_count, cycle, chunks,
    counts_ref, assignment_ref, loader_ref, q_ref, k_ref, v_ref, g_ref, q_gain_ref, k_gain_ref,
    *rest,
):
    packed_refs, boundary_ref, weight_ref = rest[:chunks], rest[chunks], rest[chunks + 1]
    step = pl.program_id(0)
    rows, width = q_ref.shape

    @pl.when(step == 0)
    def _():
        boundary, weight_first, weight_last = group_table(
            counts_ref[...], assignment_ref[...], loader_ref[...], lax.axis_index(("z", "yc")), group_count
        )
        boundary_ref[0] = boundary
        weight_ref[0:1, :] = jnp.broadcast_to(weight_first, (1, 128))
        weight_ref[1:2, :] = jnp.broadcast_to(weight_last, (1, 128))

    own_first = lax.axis_index("blk") * (rows * pl.num_programs(0)) + step * rows
    position = own_first + lax.broadcasted_iota(jnp.int32, (rows, 1), 0)
    row_weight = jnp.where(position < boundary_ref[0], weight_ref[0:1, 0:1], weight_ref[1:2, 0:1])
    q_normed = (unit_of(q_ref[...])[0] * q_gain_ref[...]).astype(jnp.bfloat16)
    k_normed = (unit_of(k_ref[...])[0] * k_gain_ref[...]).astype(jnp.bfloat16)
    g_weighted = (g_ref[...].astype(jnp.float32) * row_weight).astype(jnp.bfloat16)
    share = width // cycle
    piece = share // chunks
    for a, array in enumerate((q_normed, k_normed, v_ref[...], g_weighted)):
        for d in range(cycle):
            for c in range(chunks):
                start = d * share + c * piece
                packed_refs[c][d, a] = array[:, start : start + piece]


def pack(q_raw, k_raw, values, grad_out, q_gain, k_gain, counts, assignment, loader, cycle, group_count, chunks):
    rows, width = q_raw.shape
    piece = width // cycle // chunks
    row_block = pl.BlockSpec((ROW_STEP, width), lambda i: (i, 0))
    table = pl.BlockSpec(counts.shape, lambda i: (0, 0))
    gain = pl.BlockSpec((1, width), lambda i: (0, 0))
    out = pl.pallas_call(
        functools.partial(pack_kernel, group_count, cycle, chunks),
        grid=(rows // ROW_STEP,),
        in_specs=[table] * 3 + [row_block] * 4 + [gain] * 2,
        out_specs=[pl.BlockSpec((cycle, 4, ROW_STEP, piece), lambda i: (0, 0, i, 0))] * chunks
        + [pl.BlockSpec(memory_space=pltpu.SMEM)],
        out_shape=[jax.ShapeDtypeStruct((cycle, 4, rows, piece), jnp.bfloat16)] * chunks
        + [jax.ShapeDtypeStruct((1,), jnp.int32)],
        scratch_shapes=[pltpu.VMEM((8, 128), jnp.float32)],
        compiler_params=pltpu.CompilerParams(vmem_limit_bytes=32 * 1024 * 1024),
        cost_estimate=pl.CostEstimate(flops=12 * rows * width, bytes_accessed=16 * rows * width, transcendentals=rows),
        name="pack",
    )(counts, assignment, loader, q_raw, k_raw, values, grad_out, q_gain, k_gain)
    return out[:chunks], out[chunks]


def dot(a, b, a_dim, b_dim):
    return lax.dot_general(a, b, (((a_dim,), (b_dim,)), ((), ())), preferred_element_type=jnp.float32)


def attention_kernel(boundary_ref, x_ref, o_ref, part_ref):
    cycle, _, rows, width = x_ref.shape
    slots = cycle * rows
    scale = HEAD_DIM ** (-0.5)
    boundary = boundary_ref[0]
    q, k, v, g = (x_ref[:, a].reshape(slots, width) for a in range(4))
    key_first = lax.broadcasted_iota(jnp.int32, (slots, slots), 0) < boundary
    query_first = lax.broadcasted_iota(jnp.int32, (slots, slots), 1) < boundary
    scores = jnp.where(key_first == query_first, dot(k, q, 1, 1), masked_score)
    top = jnp.max(scores, axis=0, keepdims=True)
    powers = jnp.exp2((scores - top) * (scale * log2_e))
    softmax = powers * (1.0 / jnp.sum(powers, axis=0, keepdims=True))
    softmax_half = softmax.astype(jnp.bfloat16)
    both = dot(jnp.concatenate([v, k], axis=1), softmax_half, 0, 0)
    attended_t, key_mean_t = both[:width], both[width:]
    grad_scores = dot(v, g, 1, 1)
    row_delta = jnp.sum(g.astype(jnp.float32).T * attended_t, axis=0, keepdims=True)
    weighted_half = (softmax * grad_scores).astype(jnp.bfloat16)
    score_grad_half = (softmax * (grad_scores - row_delta)).astype(jnp.bfloat16)
    query_grad = (scale * (dot(k, weighted_half, 0, 0) - row_delta * key_mean_t)).T
    key_grad = scale * dot(score_grad_half, q, 1, 0)
    value_grad = dot(softmax_half, g, 1, 0)
    for a, array in enumerate((attended_t.T, query_grad, key_grad, value_grad)):
        o_ref[:, a] = array.astype(jnp.bfloat16).reshape(cycle, rows, width)
    part_ref[0] = jnp.concatenate(
        [
            jnp.sum(query_grad * q.astype(jnp.float32), axis=0, keepdims=True),
            jnp.sum(key_grad * k.astype(jnp.float32), axis=0, keepdims=True),
        ],
        axis=0,
    )


def attention(boundary, packed):
    cycle, kinds, rows, piece = packed.shape
    heads = piece // HEAD_DIM
    slots = cycle * rows
    block = pl.BlockSpec((cycle, kinds, rows, HEAD_DIM), lambda h: (0, 0, 0, h))
    return pl.pallas_call(
        attention_kernel,
        grid=(heads,),
        in_specs=[pl.BlockSpec(memory_space=pltpu.SMEM), block],
        out_specs=[block, pl.BlockSpec((1, 2, HEAD_DIM), lambda h: (h, 0, 0))],
        out_shape=[
            jax.ShapeDtypeStruct(packed.shape, jnp.bfloat16),
            jax.ShapeDtypeStruct((heads, 2, HEAD_DIM), jnp.float32),
        ],
        compiler_params=pltpu.CompilerParams(vmem_limit_bytes=48 * 1024 * 1024),
        cost_estimate=pl.CostEstimate(
            flops=14 * heads * slots * slots * HEAD_DIM, bytes_accessed=32 * slots * piece,
            transcendentals=heads * slots * slots,
        ),
        name="attention",
    )(boundary, packed)


def finish_kernel(cycle, chunks, *refs):
    back_refs = refs[:chunks]
    q_ref, k_ref, q_gain_ref, k_gain_ref, att_ref, dq_ref, dk_ref, dv_ref = refs[chunks:]

    def whole(a):
        return jnp.concatenate([back_refs[c][d, a] for d in range(cycle) for c in range(chunks)], axis=1)

    def norm_back(grad_normed, raw, gain):
        unit, inverse = unit_of(raw)
        grad_unit = grad_normed.astype(jnp.float32) * gain
        mean = jnp.mean(grad_unit * unit, axis=-1, keepdims=True)
        return (inverse * (grad_unit - unit * mean)).astype(jnp.bfloat16)

    att_ref[...] = whole(0)
    dq_ref[...] = norm_back(whole(1), q_ref[...], q_gain_ref[...])
    dk_ref[...] = norm_back(whole(2), k_ref[...], k_gain_ref[...])
    dv_ref[...] = whole(3)


def finish(back, q_raw, k_raw, q_gain, k_gain):
    rows, width = q_raw.shape
    cycle, kinds, _, piece = back[0].shape
    row_block = pl.BlockSpec((ROW_STEP, width), lambda i: (i, 0))
    gain = pl.BlockSpec((1, width), lambda i: (0, 0))
    return pl.pallas_call(
        functools.partial(finish_kernel, cycle, len(back)),
        grid=(rows // ROW_STEP,),
        in_specs=[pl.BlockSpec((cycle, kinds, ROW_STEP, piece), lambda i: (0, 0, i, 0))] * len(back)
        + [row_block] * 2 + [gain] * 2,
        out_specs=[row_block] * 4,
        out_shape=[jax.ShapeDtypeStruct((rows, width), jnp.bfloat16)] * 4,
        compiler_params=pltpu.CompilerParams(vmem_limit_bytes=32 * 1024 * 1024),
        cost_estimate=pl.CostEstimate(flops=20 * rows * width, bytes_accessed=20 * rows * width, transcendentals=rows),
        name="finish",
    )(*back, q_raw, k_raw, q_gain, k_gain)


def swap(array, axes):
    return lax.all_to_all(array, axes, 0, 0, tiled=True)


CHUNKS = 2


def body(q_raw, k_raw, values, grad_out, q_gain, k_gain, patch_counts, assignment, loader_shard):
    width = q_raw.shape[1]
    cycle, outer, inner = (lax.axis_size(name) for name in ("blk", "z", "yc"))
    q_gain_row, k_gain_row = q_gain.reshape(1, width), k_gain.reshape(1, width)
    tables = (x.reshape(-1, 128) for x in (patch_counts, assignment, loader_shard))
    packed, boundary = pack(
        q_raw, k_raw, values, grad_out, q_gain_row, k_gain_row, *tables, cycle, outer * inner, CHUNKS
    )
    arrived = [swap(x, "blk") for x in packed]
    results = [attention(boundary, x) for x in arrived]
    back = [swap(x, "blk") for x, _ in results]
    part = jnp.concatenate([p for _, p in results], axis=0)
    count = part.size
    part = part.reshape(1, count // 128, 128)
    part = swap(jnp.broadcast_to(part, (inner,) + part.shape[1:]), "yc")
    part = jnp.sum(part, axis=0, keepdims=True)
    part = swap(jnp.broadcast_to(part, (outer * cycle,) + part.shape[1:]), ("z", "blk"))
    part = jnp.sum(part.reshape(outer, cycle, -1, 2, 128), axis=0)
    q_gain_grad = part[:, :, 0].reshape(width) / q_gain
    k_gain_grad = part[:, :, 1].reshape(width) / k_gain
    return (*finish(back, q_raw, k_raw, q_gain_row, k_gain_row), q_gain_grad, k_gain_grad)


def solution(mesh):
    groups = mesh.shape["dp"]
    inner = min(16, groups)
    split = Mesh(
        mesh.devices.reshape(mesh.shape["blk"], groups // inner, inner), ("blk", "z", "yc")
    )
    rows = P(("z", "yc", "blk"), None)
    return jax.shard_map(
        body,
        mesh=split,
        in_specs=(rows,) * 4 + (P(),) * 5,
        out_specs=(rows,) * 4 + (P(),) * 2,
        check_vma=False,
    )
```

```python
import functools
import math

import jax
import jax.numpy as jnp
from jax import lax
from jax.experimental import pallas as pl
from jax.experimental.pallas import tpu as pltpu
from jax.sharding import Mesh, PartitionSpec as P

HEAD_DIM = 128
KINDS = 4
ROW_STEP = 64
HEAD_STEP = 2
KEY_STEP = 64
PART_ROWS = 32
GROUP_AXES = ("z", "y", "c")
MIB = 1024 * 1024

epsilon = 1e-06
masked_score = -1e30
log2_e = 1.4426950408889634


def whole_block(shape):
    return pl.BlockSpec(shape, lambda: (0,) * len(shape))


def sum_all(array):
    return jnp.sum(jnp.sum(array, axis=1, keepdims=True), axis=0, keepdims=True)


def group_table(counts, assignment, loader, group_index, group_count):
    shape = counts.shape
    entries = lax.broadcasted_iota(jnp.int32, shape, 0) * shape[1] + lax.broadcasted_iota(
        jnp.int32, shape, 1
    )
    living = counts > 0
    owned = living & (assignment == group_index)
    total = shape[0] * shape[1]
    first = jnp.where(owned, entries, total)
    first = jnp.min(jnp.min(first, axis=1, keepdims=True), axis=0, keepdims=True)
    last = jnp.where(owned, entries, -1)
    last = jnp.max(jnp.max(last, axis=1, keepdims=True), axis=0, keepdims=True)
    boundary = sum_all(jnp.where(entries == first, counts, 0))
    living_total = sum_all(living.astype(jnp.int32))

    def weight_of(entry):
        shard = sum_all(jnp.where(entries == entry, loader, 0))
        shared = sum_all((living & (loader == shard)).astype(jnp.int32))
        return living_total.astype(jnp.float32) / (group_count * shared).astype(jnp.float32)

    return boundary, weight_of(first), weight_of(last)


def pack_kernel(group_count, cycle, *refs):
    small, large = refs[:5], refs[5:9]
    packed_ref, boundary_ref = refs[9:11]
    small_held = refs[11:16]
    large_held, packed_held, small_sems, large_sems, out_sems = refs[16:]
    rows, width = large[0].shape
    steps = rows // ROW_STEP
    heads = width // cycle // HEAD_DIM
    small_copies = [pltpu.make_async_copy(small[n], small_held[n], small_sems.at[n]) for n in range(5)]
    for copy in small_copies:
        copy.start()

    def large_copy(n, step):
        block = pl.ds(step * ROW_STEP, ROW_STEP)
        return pltpu.make_async_copy(large[n].at[block], large_held.at[n, block], large_sems.at[n, step])

    def out_copy(d, step):
        block = pl.ds(step * ROW_STEP, ROW_STEP)
        return pltpu.make_async_copy(
            packed_held.at[d, :, :, block], packed_ref.at[d, :, :, block], out_sems.at[d, step]
        )

    for step in range(steps):
        for n in range(KINDS):
            large_copy(n, step).start()
    for copy in small_copies:
        copy.wait()
    boundary, weight_first, weight_last = group_table(
        small_held[0][...], small_held[1][...], small_held[2][...], lax.axis_index(GROUP_AXES), group_count
    )
    boundary_ref[...] = jnp.broadcast_to(boundary, boundary_ref.shape)
    for step in range(steps):
        block = slice(step * ROW_STEP, (step + 1) * ROW_STEP)
        position = (
            lax.axis_index("blk") * rows + step * ROW_STEP
            + lax.broadcasted_iota(jnp.int32, (ROW_STEP, 1), 0)
        )
        row_weight = jnp.where(position < boundary, weight_first, weight_last)
        for n in range(KINDS):
            large_copy(n, step).wait()
            array = large_held[n, block]
            if n < 2:
                widened = array.astype(jnp.float32)
                inverse = lax.rsqrt(jnp.mean(widened * widened, axis=-1, keepdims=True) + epsilon)
                array = (widened * inverse * small_held[3 + n][...]).astype(jnp.bfloat16)
            if n == 3:
                array = (array.astype(jnp.float32) * row_weight).astype(jnp.bfloat16)
            for d in range(cycle):
                for h in range(heads):
                    start = (d * heads + h) * HEAD_DIM
                    packed_held[d, h, n, block] = array[:, start : start + HEAD_DIM]
        for d in range(cycle):
            out_copy(d, step).start()
    for step in range(steps):
        for d in range(cycle):
            out_copy(d, step).wait()


def pack(q_raw, k_raw, values, grad_out, q_gain, k_gain, counts, assignment, loader, cycle, group_count):
    rows, width = q_raw.shape
    packed = jax.ShapeDtypeStruct((cycle, width // cycle // HEAD_DIM, KINDS, rows, HEAD_DIM), jnp.bfloat16)
    small = (counts, assignment, loader, q_gain, k_gain)
    return pl.pallas_call(
        functools.partial(pack_kernel, group_count, cycle),
        in_specs=[pl.BlockSpec(memory_space=pl.ANY)] * 9,
        out_specs=[pl.BlockSpec(memory_space=pl.ANY), pl.BlockSpec(memory_space=pltpu.VMEM)],
        out_shape=[packed, jax.ShapeDtypeStruct((8, 128), jnp.int32)],
        scratch_shapes=[pltpu.VMEM(x.shape, x.dtype) for x in small]
        + [
            pltpu.VMEM((KINDS, rows, width), jnp.bfloat16),
            pltpu.VMEM(packed.shape, packed.dtype),
            pltpu.SemaphoreType.DMA((5,)),
            pltpu.SemaphoreType.DMA((KINDS, rows // ROW_STEP)),
            pltpu.SemaphoreType.DMA((cycle, rows // ROW_STEP)),
        ],
        compiler_params=pltpu.CompilerParams(vmem_limit_bytes=60 * MIB),
        cost_estimate=pl.CostEstimate(flops=12 * rows * width, bytes_accessed=16 * rows * width, transcendentals=rows),
        name="pack",
    )(*small, q_raw, k_raw, values, grad_out)


def dot(a, b, a_dim, b_dim):
    return lax.dot_general(a, b, (((a_dim,), (b_dim,)), ((), ())), preferred_element_type=jnp.float32)


def fold(array, op):
    return op(array.reshape(-1, 8, array.shape[-1]), axis=0)


def attention_kernel(cycle, boundary_ref, x_ref, *rest):
    o_refs, part_ref = rest[:cycle], rest[cycle]
    side_ref, score_ref, grad_ref, softmax_ref, weighted_ref, score_grad_ref, held_ref = rest[cycle + 1 :]
    _, heads, kinds, rows, width = x_ref.shape
    slots = cycle * rows
    scale = HEAD_DIM ** (-0.5)
    boundary = boundary_ref[0:1, 0:1]
    step = pl.program_id(0)
    place = lax.axis_index("blk")
    key_steps = [slice(j, j + KEY_STEP) for j in range(0, slots, KEY_STEP)]
    query_side = (lax.broadcasted_iota(jnp.int32, (1, slots), 1) < boundary).astype(jnp.int32)

    @pl.when(step == 0)
    def _():
        side_ref[...] = (lax.broadcasted_iota(jnp.int32, side_ref.shape, 0) < boundary).astype(jnp.int32)

    def operands(h):
        return [x_ref[:, h, a].reshape(slots, width) for a in range(kinds)]

    def products(h):
        q, k, v, g = operands(h)
        scores = dot(k, q, 1, 1)
        top = None
        for down in key_steps:
            side = jnp.concatenate([side_ref[down]] * (slots // 128), axis=1)
            block = jnp.where(side == query_side, scores[down], masked_score)
            score_ref[h, down] = block
            block = fold(block, jnp.max)
            top = block if top is None else jnp.maximum(top, block)
        grad_ref[h] = dot(v, g, 1, 1)
        return jnp.max(top, axis=0, keepdims=True)

    def weights(h, top):
        total = 0.0
        for down in key_steps:
            block = jnp.exp2((score_ref[h, down] - top) * (scale * log2_e))
            score_ref[h, down] = block
            total += fold(block, jnp.sum)
        inverse = 1.0 / jnp.sum(total, axis=0, keepdims=True)
        row_delta = 0.0
        for down in key_steps:
            softmax = score_ref[h, down] * inverse
            weighted = softmax * grad_ref[h, down]
            row_delta += fold(weighted, jnp.sum)
            softmax_ref[h, down] = softmax.astype(jnp.bfloat16)
            weighted_ref[h, down] = weighted.astype(jnp.bfloat16)
        row_delta = jnp.sum(row_delta, axis=0, keepdims=True)
        for down in key_steps:
            softmax = score_ref[h, down] * inverse
            score_grad_ref[h, down] = (softmax * (grad_ref[h, down] - row_delta)).astype(jnp.bfloat16)
        return row_delta

    def results(h, row_delta):
        q, k, v, g = operands(h)
        both = dot(jnp.concatenate([v, k], axis=1), softmax_ref[h], 0, 0)
        query_grad = (scale * (dot(k, weighted_ref[h], 0, 0) - row_delta * both[width:])).T
        key_grad = scale * dot(score_grad_ref[h], q, 1, 0)
        held_ref[h, 0] = both[:width].T.astype(jnp.bfloat16)
        held_ref[h, 1] = query_grad.astype(jnp.bfloat16)
        held_ref[h, 2] = key_grad.astype(jnp.bfloat16)
        held_ref[h, 3] = dot(softmax_ref[h], g, 1, 0).astype(jnp.bfloat16)
        for s in range(cycle):
            first = pl.multiple_of(lax.rem(place + cycle - s, cycle) * rows, rows)
            o_refs[s][h] = held_ref[h, :, pl.ds(first, rows), :]
        query_part = jnp.sum(query_grad * q.astype(jnp.float32), axis=0, keepdims=True)
        key_part = jnp.sum(key_grad * k.astype(jnp.float32), axis=0, keepdims=True)
        parts = jnp.concatenate([query_part, key_part], axis=0)
        at = pl.ds(2 * (step * heads + h), 2)
        part_ref[:, at, :] = jnp.broadcast_to(parts, (part_ref.shape[0], 2, width))

    top = products(0)
    for h in range(heads):
        row_delta = weights(h, top)
        if h + 1 < heads:
            top = products(h + 1)
        results(h, row_delta)


def attention(boundary, arrived, copies):
    cycle, heads, kinds, rows, width = arrived.shape
    slots = cycle * rows
    parts = (copies, PART_ROWS, width)
    square = (HEAD_STEP, slots, slots)
    out = pl.pallas_call(
        functools.partial(attention_kernel, cycle),
        grid=(heads // HEAD_STEP,),
        in_specs=[
            pl.BlockSpec(boundary.shape, lambda h: (0, 0)),
            pl.BlockSpec((cycle, HEAD_STEP, kinds, rows, width), lambda h: (0, h, 0, 0, 0)),
        ],
        out_specs=[pl.BlockSpec((HEAD_STEP, kinds, rows, width), lambda h: (h, 0, 0, 0))] * cycle
        + [pl.BlockSpec(parts, lambda h: (0, 0, 0))],
        out_shape=[jax.ShapeDtypeStruct((heads, kinds, rows, width), jnp.bfloat16)] * cycle
        + [jax.ShapeDtypeStruct(parts, jnp.float32)],
        scratch_shapes=[
            pltpu.VMEM((slots, 128), jnp.int32),
            pltpu.VMEM(square, jnp.float32),
            pltpu.VMEM(square, jnp.float32),
            pltpu.VMEM(square, jnp.bfloat16),
            pltpu.VMEM(square, jnp.bfloat16),
            pltpu.VMEM(square, jnp.bfloat16),
            pltpu.VMEM((HEAD_STEP, kinds, slots, width), jnp.bfloat16),
        ],
        compiler_params=pltpu.CompilerParams(vmem_limit_bytes=32 * MIB),
        cost_estimate=pl.CostEstimate(
            flops=14 * heads * slots * slots * width, bytes_accessed=16 * slots * width * heads,
            transcendentals=heads * slots * slots,
        ),
        name="attention",
    )(boundary, arrived)
    return out[:cycle], out[cycle]


def finish_kernel(cycle, *refs):
    back_refs, raws, gains = refs[:cycle], refs[cycle : cycle + 2], refs[cycle + 2 : cycle + 4]
    att_ref, dq_ref, dk_ref, dv_ref = refs[cycle + 4 : cycle + 8]
    raw_held, grad_held, raw_sems, grad_sems, copy_sems = refs[cycle + 8 :]
    heads, kinds, rows, _ = back_refs[0].shape
    share = heads * HEAD_DIM
    width = share * cycle
    steps = rows // ROW_STEP
    place = lax.axis_index("blk")
    starts = [pl.multiple_of(lax.rem(place + s, cycle) * share, share) for s in range(cycle)]

    def raw_copy(n, step):
        block = pl.ds(step * ROW_STEP, ROW_STEP)
        return pltpu.make_async_copy(raws[n].at[block], raw_held.at[n, block], raw_sems.at[n, step])

    def grad_copy(n, step):
        block = pl.ds(step * ROW_STEP, ROW_STEP)
        return pltpu.make_async_copy(
            grad_held.at[n, block], (dq_ref, dk_ref)[n].at[block], grad_sems.at[n, step]
        )

    def plain_copy(n, s, h):
        target = (att_ref, dv_ref)[n].at[:, pl.ds(starts[s] + h * HEAD_DIM, HEAD_DIM)]
        return pltpu.make_async_copy(back_refs[s].at[h, 3 * n], target, copy_sems.at[n, s, h])

    plain = [plain_copy(n, s, h) for n in range(2) for s in range(cycle) for h in range(heads)]
    for step in range(steps):
        for n in range(2):
            raw_copy(n, step).start()
    for copy in plain:
        copy.start()
    for step in range(steps):
        block = slice(step * ROW_STEP, (step + 1) * ROW_STEP)
        for n in range(2):
            raw_copy(n, step).wait()
            raw = [raw_held[n, block, pl.ds(start, share)].astype(jnp.float32) for start in starts]
            grad = [
                jnp.concatenate([back[h, 1 + n, block] for h in range(heads)], axis=1).astype(jnp.float32)
                * gains[n][:, pl.ds(start, share)]
                for back, start in zip(back_refs, starts)
            ]
            square = sum(jnp.sum(x * x, axis=-1, keepdims=True) for x in raw)
            along = sum(jnp.sum(x * y, axis=-1, keepdims=True) for x, y in zip(raw, grad))
            inverse = lax.rsqrt(square / width + epsilon)
            along = along * inverse * inverse / width
            for x, y, start in zip(raw, grad, starts):
                grad_held[n, block, pl.ds(start, share)] = (inverse * (y - x * along)).astype(jnp.bfloat16)
            grad_copy(n, step).start()
    for copy in plain:
        copy.wait()
    for step in range(steps):
        for n in range(2):
            grad_copy(n, step).wait()


def finish(back, q_raw, k_raw, q_gain, k_gain):
    rows, width = q_raw.shape
    cycle = len(back)
    heads = back[0].shape[0]
    steps = rows // ROW_STEP
    return pl.pallas_call(
        functools.partial(finish_kernel, cycle),
        in_specs=[whole_block(back[0].shape)] * cycle
        + [pl.BlockSpec(memory_space=pl.ANY)] * 2
        + [whole_block((1, width))] * 2,
        out_specs=[pl.BlockSpec(memory_space=pl.ANY)] * 4,
        out_shape=[jax.ShapeDtypeStruct((rows, width), jnp.bfloat16)] * 4,
        scratch_shapes=[
            pltpu.VMEM((2, rows, width), jnp.bfloat16),
            pltpu.VMEM((2, rows, width), jnp.bfloat16),
            pltpu.SemaphoreType.DMA((2, steps)),
            pltpu.SemaphoreType.DMA((2, steps)),
            pltpu.SemaphoreType.DMA((2, cycle, heads)),
        ],
        compiler_params=pltpu.CompilerParams(vmem_limit_bytes=32 * MIB),
        cost_estimate=pl.CostEstimate(flops=20 * rows * width, bytes_accessed=20 * rows * width, transcendentals=rows),
        name="finish",
    )(*back, q_raw, k_raw, q_gain, k_gain)


def respread_kernel(part_ref, o_ref):
    o_ref[...] = jnp.broadcast_to(jnp.sum(part_ref[...], axis=0, keepdims=True), o_ref.shape)


def respread(part, copies):
    out_shape = (copies,) + part.shape[1:]
    return pl.pallas_call(
        respread_kernel,
        in_specs=[whole_block(part.shape)],
        out_specs=whole_block(out_shape),
        out_shape=jax.ShapeDtypeStruct(out_shape, jnp.float32),
        compiler_params=pltpu.CompilerParams(vmem_limit_bytes=32 * MIB),
        name="respread",
    )(part)


def gain_grad_kernel(part_ref, q_gain_ref, k_gain_ref, q_ref, k_ref):
    cycle, count, _ = part_ref.shape
    for n, (gain_ref, out_ref) in enumerate(((q_gain_ref, q_ref), (k_gain_ref, k_ref))):
        rows = jnp.concatenate(
            [part_ref[d, 2 * h + n : 2 * h + n + 1] for d in range(cycle) for h in range(count // 2)], axis=0
        )
        out_ref[...] = rows / gain_ref[...]


def gain_grad(part, q_gain, k_gain):
    shape = (q_gain.size // 128, 128)
    out = pl.pallas_call(
        gain_grad_kernel,
        in_specs=[whole_block(part.shape)] + [whole_block(shape)] * 2,
        out_specs=[whole_block(shape)] * 2,
        out_shape=[jax.ShapeDtypeStruct(shape, jnp.float32)] * 2,
        compiler_params=pltpu.CompilerParams(vmem_limit_bytes=32 * MIB),
        name="gain_grad",
    )(part, q_gain.reshape(shape), k_gain.reshape(shape))
    return [x.reshape(-1) for x in out]


def swap(array, axes):
    return lax.all_to_all(array, axes, 0, 0, tiled=True)


def body(q_raw, k_raw, values, grad_out, q_gain, k_gain, patch_counts, assignment, loader_shard):
    width = q_raw.shape[1]
    cycle, outer, inner, cores = (lax.axis_size(name) for name in ("blk", *GROUP_AXES))
    q_gain_row, k_gain_row = q_gain.reshape(1, width), k_gain.reshape(1, width)
    tables = (x.reshape(-1, 128) for x in (patch_counts, assignment, loader_shard))
    packed, boundary = pack(
        q_raw, k_raw, values, grad_out, q_gain_row, k_gain_row, *tables, cycle, outer * inner * cores
    )
    slots, part = attention(boundary, swap(packed, "blk"), inner * cores)
    back = [slots[0]] + [
        lax.ppermute(slots[s], "blk", [(i, (i - s) % cycle) for i in range(cycle)]) for s in range(1, cycle)
    ]

    part = respread(swap(part, ("y", "c"))[:, : 2 * slots[0].shape[0]], outer)
    part = respread(swap(part, "z"), cycle)
    part = swap(part, "blk")
    return (*finish(back, q_raw, k_raw, q_gain_row, k_gain_row), *gain_grad(part, q_gain, k_gain))


def solution(mesh):
    groups = mesh.shape["dp"]
    cores = math.gcd(groups, 2)
    inner = math.gcd(groups // cores, 8)
    split = Mesh(
        mesh.devices.reshape(mesh.shape["blk"], groups // cores // inner, inner, cores), ("blk", *GROUP_AXES)
    )
    rows = P((*GROUP_AXES, "blk"), None)
    return jax.shard_map(
        body,
        mesh=split,
        in_specs=(rows,) * 4 + (P(),) * 5,
        out_specs=(rows,) * 4 + (P(),) * 2,
        check_vma=False,
    )
```

```python
import functools
import math

import jax
import jax.numpy as jnp
from jax import lax
from jax.experimental import pallas as pl
from jax.experimental.pallas import tpu as pltpu
from jax.sharding import Mesh, PartitionSpec as P

HEAD_DIM = 128
KINDS = 4
PACK_STEP = 128
ROW_STEP = 64
HEAD_STEP = 2
KEY_STEP = 64
PART_ROWS = 32
GROUP_AXES = ("z", "y", "c")
MIB = 1024 * 1024

epsilon = 1e-06
masked_score = -1e30
log2_e = 1.4426950408889634


def whole_block(shape):
    return pl.BlockSpec(memory_space=pltpu.VMEM)


def sum_all(array):
    return jnp.sum(jnp.sum(array, axis=1, keepdims=True), axis=0, keepdims=True)


def group_table(counts, assignment, loader, group_index, group_count):
    shape = counts.shape
    entries = lax.broadcasted_iota(jnp.int32, shape, 0) * shape[1] + lax.broadcasted_iota(
        jnp.int32, shape, 1
    )
    living = counts > 0
    owned = living & (assignment == group_index)
    total = shape[0] * shape[1]
    first = jnp.where(owned, entries, total)
    first = jnp.min(jnp.min(first, axis=1, keepdims=True), axis=0, keepdims=True)
    last = jnp.where(owned, entries, -1)
    last = jnp.max(jnp.max(last, axis=1, keepdims=True), axis=0, keepdims=True)
    boundary = sum_all(jnp.where(entries == first, counts, 0))
    living_total = sum_all(living.astype(jnp.int32))

    def weight_of(entry):
        shard = sum_all(jnp.where(entries == entry, loader, 0))
        shared = sum_all((living & (loader == shard)).astype(jnp.int32))
        return living_total.astype(jnp.float32) / (group_count * shared).astype(jnp.float32)

    return boundary, weight_of(first), weight_of(last)


def pack_kernel(group_count, cycle, *refs):
    small, large = refs[:5], refs[5:9]
    packed_ref, boundary_ref = refs[9:11]
    small_held = refs[11:16]
    large_held, packed_held, boundary_held, small_sems, large_sems, out_sems, boundary_sem = refs[16:]
    boundary_copy = pltpu.make_async_copy(boundary_held, boundary_ref, boundary_sem)
    rows, width = large[0].shape
    steps = rows // PACK_STEP
    heads = width // cycle // HEAD_DIM
    small_copies = [pltpu.make_async_copy(small[n], small_held[n], small_sems.at[n]) for n in range(5)]
    for copy in small_copies:
        copy.start()

    def large_copy(n, step):
        block = pl.ds(step * PACK_STEP, PACK_STEP)
        return pltpu.make_async_copy(large[n].at[block], large_held.at[n, block], large_sems.at[n, step])

    def out_copies(n):
        if n == 2:
            return [
                pltpu.make_async_copy(
                    large_held.at[2, :, pl.ds((d * heads + h) * HEAD_DIM, HEAD_DIM)],
                    packed_ref.at[d, h, 2],
                    out_sems.at[d, KINDS + h],
                )
                for d in range(cycle)
                for h in range(heads)
            ]
        return [
            pltpu.make_async_copy(packed_held.at[d, :, n], packed_ref.at[d, :, n], out_sems.at[d, n])
            for d in range(cycle)
        ]

    order = (2, 0, 1, 3)
    for n in order:
        for step in range(steps):
            large_copy(n, step).start()
    for n in order:
        if n == 0:
            for copy in small_copies[3:]:
                copy.wait()
        if n == 3:
            for copy in small_copies[:3]:
                copy.wait()
            boundary, weight_first, weight_last = group_table(
                small_held[0][...], small_held[1][...], small_held[2][...], lax.axis_index(GROUP_AXES), group_count
            )
            boundary_held[...] = jnp.broadcast_to(boundary, boundary_held.shape)
            boundary_copy.start()
        for step in range(steps):
            block = slice(step * PACK_STEP, (step + 1) * PACK_STEP)
            large_copy(n, step).wait()
            array = large_held[n, block]
            if n < 2:
                widened = array.astype(jnp.float32)
                inverse = lax.rsqrt(jnp.mean(widened * widened, axis=-1, keepdims=True) + epsilon)
                array = (widened * inverse * small_held[3 + n][...]).astype(jnp.bfloat16)
            if n == 3:
                position = (
                    lax.axis_index("blk") * rows + step * PACK_STEP
                    + lax.broadcasted_iota(jnp.int32, (PACK_STEP, 1), 0)
                )
                row_weight = jnp.where(position < boundary, weight_first, weight_last)
                array = (array.astype(jnp.float32) * row_weight).astype(jnp.bfloat16)
            if n == 2:
                continue
            for d in range(cycle):
                for h in range(heads):
                    start = (d * heads + h) * HEAD_DIM
                    packed_held[d, h, n, block] = array[:, start : start + HEAD_DIM]
        for copy in out_copies(n):
            copy.start()
    for n in order:
        for copy in out_copies(n):
            copy.wait()
    boundary_copy.wait()


def pack(q_raw, k_raw, values, grad_out, q_gain, k_gain, counts, assignment, loader, cycle, group_count):
    rows, width = q_raw.shape
    packed = jax.ShapeDtypeStruct((cycle, width // cycle // HEAD_DIM, KINDS, rows, HEAD_DIM), jnp.bfloat16)
    small = (counts, assignment, loader, q_gain, k_gain)
    return pl.pallas_call(
        functools.partial(pack_kernel, group_count, cycle),
        in_specs=[pl.BlockSpec(memory_space=pl.ANY)] * 9,
        out_specs=[pl.BlockSpec(memory_space=pl.ANY)] * 2,
        out_shape=[packed, jax.ShapeDtypeStruct((8, 128), jnp.int32)],
        scratch_shapes=[pltpu.VMEM(x.shape, x.dtype) for x in small]
        + [
            pltpu.VMEM((KINDS, rows, width), jnp.bfloat16),
            pltpu.VMEM(packed.shape, packed.dtype),
            pltpu.VMEM((8, 128), jnp.int32),
            pltpu.SemaphoreType.DMA((5,)),
            pltpu.SemaphoreType.DMA((KINDS, rows // PACK_STEP)),
            pltpu.SemaphoreType.DMA((cycle, KINDS + packed.shape[1])),
            pltpu.SemaphoreType.DMA(()),
        ],
        compiler_params=pltpu.CompilerParams(vmem_limit_bytes=60 * MIB),
        cost_estimate=pl.CostEstimate(flops=12 * rows * width, bytes_accessed=16 * rows * width, transcendentals=rows),
        name="pack",
    )(*small, q_raw, k_raw, values, grad_out)


def dot(a, b, a_dim, b_dim):
    return lax.dot_general(a, b, (((a_dim,), (b_dim,)), ((), ())), preferred_element_type=jnp.float32)


def fold(array, op):
    return op(array.reshape(-1, 8, array.shape[-1]), axis=0)


def attention_kernel(cycle, boundary_ref, x_ref, *rest):
    o_refs, part_ref = rest[:cycle], rest[cycle]
    side_ref, score_ref, grad_ref, softmax_ref, weighted_ref, score_grad_ref, held_ref = rest[cycle + 1 :]
    _, _, kinds, rows, width = x_ref.shape
    heads = HEAD_STEP
    slots = cycle * rows
    scale = HEAD_DIM ** (-0.5)
    boundary = boundary_ref[0:1, 0:1]
    step = pl.program_id(0)
    place = lax.axis_index("blk")
    key_steps = [slice(j, j + KEY_STEP) for j in range(0, slots, KEY_STEP)]
    query_side = (lax.broadcasted_iota(jnp.int32, (1, slots), 1) < boundary).astype(jnp.int32)

    @pl.when(step == 0)
    def _():
        side_ref[...] = (lax.broadcasted_iota(jnp.int32, side_ref.shape, 0) < boundary).astype(jnp.int32)
        part_ref[...] = jnp.zeros_like(part_ref)

    def operands(h):
        return [x_ref[:, step * heads + h, a].reshape(slots, width) for a in range(kinds)]

    def products(h):
        q, k, v, g = operands(h)
        scores = dot(k, q, 1, 1)
        top = None
        for down in key_steps:
            side = jnp.concatenate([side_ref[down]] * (slots // 128), axis=1)
            block = jnp.where(side == query_side, scores[down], masked_score)
            score_ref[h, down] = block
            block = fold(block, jnp.max)
            top = block if top is None else jnp.maximum(top, block)
        grad_ref[h] = dot(v, g, 1, 1)
        return jnp.max(top, axis=0, keepdims=True)

    def weights(h, top):
        total = 0.0
        for down in key_steps:
            block = jnp.exp2((score_ref[h, down] - top) * (scale * log2_e))
            score_ref[h, down] = block
            total += fold(block, jnp.sum)
        inverse = 1.0 / jnp.sum(total, axis=0, keepdims=True)
        row_delta = 0.0
        for down in key_steps:
            softmax = score_ref[h, down] * inverse
            weighted = softmax * grad_ref[h, down]
            row_delta += fold(weighted, jnp.sum)
            softmax_ref[h, down] = softmax.astype(jnp.bfloat16)
            weighted_ref[h, down] = weighted.astype(jnp.bfloat16)
        row_delta = jnp.sum(row_delta, axis=0, keepdims=True)
        for down in key_steps:
            softmax = score_ref[h, down] * inverse
            score_grad_ref[h, down] = (softmax * (grad_ref[h, down] - row_delta)).astype(jnp.bfloat16)
        return row_delta

    def results(h, row_delta):
        q, k, v, g = operands(h)
        both = dot(jnp.concatenate([v, k], axis=1), softmax_ref[h], 0, 0)
        query_grad = (scale * (dot(k, weighted_ref[h], 0, 0) - row_delta * both[width:])).T
        key_grad = scale * dot(score_grad_ref[h], q, 1, 0)
        held_ref[h, 0] = both[:width].T.astype(jnp.bfloat16)
        held_ref[h, 1] = query_grad.astype(jnp.bfloat16)
        held_ref[h, 2] = key_grad.astype(jnp.bfloat16)
        held_ref[h, 3] = dot(softmax_ref[h], g, 1, 0).astype(jnp.bfloat16)
        for s in range(cycle):
            first = pl.multiple_of(lax.rem(place + cycle - s, cycle) * rows, rows)
            o_refs[s][step * heads + h] = held_ref[h, :, pl.ds(first, rows), :]
        query_part = jnp.sum(query_grad * q.astype(jnp.float32), axis=0, keepdims=True)
        key_part = jnp.sum(key_grad * k.astype(jnp.float32), axis=0, keepdims=True)
        parts = jnp.concatenate([query_part, key_part], axis=0)
        at = pl.ds(2 * (step * heads + h), 2)
        part_ref[:, at, :] = jnp.broadcast_to(parts, (part_ref.shape[0], 2, width))

    top = products(0)
    for h in range(heads):
        row_delta = weights(h, top)
        if h + 1 < heads:
            top = products(h + 1)
        results(h, row_delta)


def attention(boundary, arrived, copies):
    cycle, heads, kinds, rows, width = arrived.shape
    slots = cycle * rows
    parts = (copies, PART_ROWS, width)
    square = (HEAD_STEP, slots, slots)
    out = pl.pallas_call(
        functools.partial(attention_kernel, cycle),
        grid=(heads // HEAD_STEP,),
        in_specs=[
            pl.BlockSpec(memory_space=pltpu.VMEM),
            pl.BlockSpec(memory_space=pltpu.VMEM),
        ],
        out_specs=[pl.BlockSpec(memory_space=pltpu.VMEM)] * cycle
        + [pl.BlockSpec(parts, lambda h: (0, 0, 0))],
        out_shape=[jax.ShapeDtypeStruct((heads, kinds, rows, width), jnp.bfloat16)] * cycle
        + [jax.ShapeDtypeStruct(parts, jnp.float32)],
        scratch_shapes=[
            pltpu.VMEM((slots, 128), jnp.int32),
            pltpu.VMEM(square, jnp.float32),
            pltpu.VMEM(square, jnp.float32),
            pltpu.VMEM(square, jnp.bfloat16),
            pltpu.VMEM(square, jnp.bfloat16),
            pltpu.VMEM(square, jnp.bfloat16),
            pltpu.VMEM((HEAD_STEP, kinds, slots, width), jnp.bfloat16),
        ],
        compiler_params=pltpu.CompilerParams(vmem_limit_bytes=32 * MIB),
        cost_estimate=pl.CostEstimate(
            flops=14 * heads * slots * slots * width, bytes_accessed=16 * slots * width * heads,
            transcendentals=heads * slots * slots,
        ),
        name="attention",
    )(boundary, arrived)
    return out[:cycle], out[cycle]


def slot_order(cycle):
    return sorted(range(cycle), key=lambda s: -min(s, cycle - s))


def finish_kernel(cycle, *refs):
    back_refs, raws, gains = [None] * cycle, refs[cycle : cycle + 2], refs[cycle + 2 : cycle + 4]
    for s, ref in zip(slot_order(cycle), refs):
        back_refs[s] = ref
    att_ref, dq_ref, dk_ref, dv_ref = refs[cycle + 4 : cycle + 8]
    raw_held, grad_held, raw_sems, grad_sems, copy_sems = refs[cycle + 8 :]
    heads, kinds, rows, _ = back_refs[0].shape
    share = heads * HEAD_DIM
    width = share * cycle
    steps = rows // ROW_STEP
    place = lax.axis_index("blk")
    starts = [pl.multiple_of(lax.rem(place + s, cycle) * share, share) for s in range(cycle)]

    def raw_copy(n, step):
        block = pl.ds(step * ROW_STEP, ROW_STEP)
        return pltpu.make_async_copy(raws[n].at[block], raw_held.at[n, block], raw_sems.at[n, step])

    def grad_copy(n, step):
        block = pl.ds(step * ROW_STEP, ROW_STEP)
        return pltpu.make_async_copy(
            grad_held.at[n, block], (dq_ref, dk_ref)[n].at[block], grad_sems.at[n, step]
        )

    def plain_copy(n, s, h):
        target = (att_ref, dv_ref)[n].at[:, pl.ds(starts[s] + h * HEAD_DIM, HEAD_DIM)]
        return pltpu.make_async_copy(back_refs[s].at[h, 3 * n], target, copy_sems.at[n, s, h])

    plain = [plain_copy(n, s, h) for n in range(2) for s in range(cycle) for h in range(heads)]
    for step in range(steps):
        for n in range(2):
            raw_copy(n, step).start()
    for copy in plain:
        copy.start()
    for step in range(steps):
        block = slice(step * ROW_STEP, (step + 1) * ROW_STEP)
        for n in range(2):
            raw_copy(n, step).wait()
            raw = [raw_held[n, block, pl.ds(start, share)].astype(jnp.float32) for start in starts]
            grad = [
                jnp.concatenate([back[h, 1 + n, block] for h in range(heads)], axis=1).astype(jnp.float32)
                * gains[n][:, pl.ds(start, share)]
                for back, start in zip(back_refs, starts)
            ]
            square = sum(jnp.sum(x * x, axis=-1, keepdims=True) for x in raw)
            along = sum(jnp.sum(x * y, axis=-1, keepdims=True) for x, y in zip(raw, grad))
            inverse = lax.rsqrt(square / width + epsilon)
            along = along * inverse * inverse / width
            for x, y, start in zip(raw, grad, starts):
                grad_held[n, block, pl.ds(start, share)] = (inverse * (y - x * along)).astype(jnp.bfloat16)
            grad_copy(n, step).start()
    for copy in plain:
        copy.wait()
    for step in range(steps):
        for n in range(2):
            grad_copy(n, step).wait()


def finish(back, q_raw, k_raw, q_gain, k_gain):
    rows, width = q_raw.shape
    cycle = len(back)
    heads = back[0].shape[0]
    steps = rows // ROW_STEP
    return pl.pallas_call(
        functools.partial(finish_kernel, cycle),
        in_specs=[whole_block(back[0].shape)] * cycle
        + [pl.BlockSpec(memory_space=pl.ANY)] * 2
        + [whole_block((1, width))] * 2,
        out_specs=[pl.BlockSpec(memory_space=pl.ANY)] * 4,
        out_shape=[jax.ShapeDtypeStruct((rows, width), jnp.bfloat16)] * 4,
        scratch_shapes=[
            pltpu.VMEM((2, rows, width), jnp.bfloat16),
            pltpu.VMEM((2, rows, width), jnp.bfloat16),
            pltpu.SemaphoreType.DMA((2, steps)),
            pltpu.SemaphoreType.DMA((2, steps)),
            pltpu.SemaphoreType.DMA((2, cycle, heads)),
        ],
        compiler_params=pltpu.CompilerParams(vmem_limit_bytes=32 * MIB),
        cost_estimate=pl.CostEstimate(flops=20 * rows * width, bytes_accessed=20 * rows * width, transcendentals=rows),
        name="finish",
    )(*(back[s] for s in slot_order(cycle)), q_raw, k_raw, q_gain, k_gain)


def respread_kernel(part_ref, o_ref):
    o_ref[...] = jnp.broadcast_to(jnp.sum(part_ref[...], axis=0, keepdims=True), o_ref.shape)


def respread(part, copies):
    out_shape = (copies,) + part.shape[1:]
    return pl.pallas_call(
        respread_kernel,
        in_specs=[whole_block(part.shape)],
        out_specs=whole_block(out_shape),
        out_shape=jax.ShapeDtypeStruct(out_shape, jnp.float32),
        compiler_params=pltpu.CompilerParams(vmem_limit_bytes=32 * MIB),
        name="respread",
    )(part)


def gain_grad_kernel(part_ref, q_gain_ref, k_gain_ref, q_ref, k_ref):
    total = jnp.sum(part_ref[...], axis=0)
    cycle, count, _ = total.shape
    for n, (gain_ref, out_ref) in enumerate(((q_gain_ref, q_ref), (k_gain_ref, k_ref))):
        rows = jnp.concatenate(
            [total[d, 2 * h + n : 2 * h + n + 1] for d in range(cycle) for h in range(count // 2)], axis=0
        )
        out_ref[...] = rows / gain_ref[...]


def gain_grad(part, q_gain, k_gain):
    shape = (q_gain.size // 128, 128)
    out = pl.pallas_call(
        gain_grad_kernel,
        in_specs=[whole_block(part.shape)] + [whole_block(shape)] * 2,
        out_specs=[whole_block(shape)] * 2,
        out_shape=[jax.ShapeDtypeStruct(shape, jnp.float32)] * 2,
        compiler_params=pltpu.CompilerParams(vmem_limit_bytes=32 * MIB),
        name="gain_grad",
    )(part, q_gain.reshape(shape), k_gain.reshape(shape))
    return [x.reshape(-1) for x in out]


def swap(array, axes):
    return lax.all_to_all(array, axes, 0, 0, tiled=True)


def body(q_raw, k_raw, values, grad_out, q_gain, k_gain, patch_counts, assignment, loader_shard):
    width = q_raw.shape[1]
    cycle, outer, inner, cores = (lax.axis_size(name) for name in ("blk", *GROUP_AXES))
    q_gain_row, k_gain_row = q_gain.reshape(1, width), k_gain.reshape(1, width)
    tables = (x.reshape(-1, 128) for x in (patch_counts, assignment, loader_shard))
    packed, boundary = pack(
        q_raw, k_raw, values, grad_out, q_gain_row, k_gain_row, *tables, cycle, outer * inner * cores
    )
    slots, part = attention(boundary, swap(packed, "blk"), inner * cores)
    back = list(slots)
    for s in slot_order(cycle)[:-1]:
        back[s] = lax.ppermute(slots[s], "blk", [(i, (i - s) % cycle) for i in range(cycle)])

    part = respread(swap(part, ("y", "c"))[:, : 2 * slots[0].shape[0]], outer * cycle)
    part = swap(part, ("z", "blk"))
    part = part.reshape(outer, cycle, *part.shape[1:])
    return (*finish(back, q_raw, k_raw, q_gain_row, k_gain_row), *gain_grad(part, q_gain, k_gain))


def solution(mesh):
    groups = mesh.shape["dp"]
    cores = math.gcd(groups, 2)
    inner = math.gcd(groups // cores, 8)
    split = Mesh(
        mesh.devices.reshape(mesh.shape["blk"], groups // cores // inner, inner, cores), ("blk", *GROUP_AXES)
    )
    rows = P((*GROUP_AXES, "blk"), None)
    return jax.shard_map(
        body,
        mesh=split,
        in_specs=(rows,) * 4 + (P(),) * 5,
        out_specs=(rows,) * 4 + (P(),) * 2,
        check_vma=False,
    )
```

```python
import functools
import math

import jax
import jax.numpy as jnp
from jax import lax
from jax.experimental import pallas as pl
from jax.experimental.pallas import tpu as pltpu
from jax.sharding import Mesh, PartitionSpec as P

HEAD_DIM = 128
KINDS = 4
PACK_STEP = 128
ROW_STEP = 128
HEAD_STEP = 4
KEY_STEP = 64
PART_ROWS = 24
GROUP_AXES = ("z", "y", "c")
MIB = 1024 * 1024

epsilon = 1e-06
masked_score = -1e30
log2_e = 1.4426950408889634


def whole_block(shape):
    return pl.BlockSpec(memory_space=pltpu.VMEM)


def sum_all(array):
    return jnp.sum(jnp.sum(array, axis=1, keepdims=True), axis=0, keepdims=True)


def group_table(counts, assignment, loader, group_index, group_count):
    shape = counts.shape
    entries = lax.broadcasted_iota(jnp.int32, shape, 0) * shape[1] + lax.broadcasted_iota(
        jnp.int32, shape, 1
    )
    living = counts > 0
    owned = living & (assignment == group_index)
    total = shape[0] * shape[1]
    first = jnp.where(owned, entries, total)
    first = jnp.min(jnp.min(first, axis=1, keepdims=True), axis=0, keepdims=True)
    last = jnp.where(owned, entries, -1)
    last = jnp.max(jnp.max(last, axis=1, keepdims=True), axis=0, keepdims=True)
    boundary = sum_all(jnp.where(entries == first, counts, 0))
    living_total = sum_all(living.astype(jnp.int32))

    def weight_of(entry):
        shard = sum_all(jnp.where(entries == entry, loader, 0))
        shared = sum_all((living & (loader == shard)).astype(jnp.int32))
        return living_total.astype(jnp.float32) / (group_count * shared).astype(jnp.float32)

    return boundary, weight_of(first), weight_of(last)


def pack_kernel(group_count, cycle, *refs):
    small, large = refs[:5], refs[5:9]
    packed_ref, boundary_ref = refs[9:11]
    small_held = refs[11:16]
    large_held, packed_held, boundary_held, small_sems, large_sems, out_sems, boundary_sem = refs[16:]
    boundary_copy = pltpu.make_async_copy(boundary_held, boundary_ref, boundary_sem)
    rows, width = large[0].shape
    steps = rows // PACK_STEP
    heads = width // cycle // HEAD_DIM
    small_copies = [pltpu.make_async_copy(small[n], small_held[n], small_sems.at[n]) for n in range(5)]
    for copy in small_copies:
        copy.start()

    def large_copy(n, step):
        block = pl.ds(step * PACK_STEP, PACK_STEP)
        return pltpu.make_async_copy(large[n].at[block], large_held.at[n, block], large_sems.at[n, step])

    def out_copies(n):
        if n == 2:
            return [
                pltpu.make_async_copy(
                    large_held.at[2, :, pl.ds((d * heads + h) * HEAD_DIM, HEAD_DIM)],
                    packed_ref.at[d, h, 2],
                    out_sems.at[d, KINDS + h],
                )
                for d in range(cycle)
                for h in range(heads)
            ]
        return [
            pltpu.make_async_copy(packed_held.at[d, :, n], packed_ref.at[d, :, n], out_sems.at[d, n])
            for d in range(cycle)
        ]

    order = (2, 0, 1, 3)
    for n in order:
        for step in range(steps):
            large_copy(n, step).start()
    for n in order:
        if n == 0:
            for copy in small_copies[3:]:
                copy.wait()
        if n == 3:
            for copy in small_copies[:3]:
                copy.wait()
            boundary, weight_first, weight_last = group_table(
                small_held[0][...], small_held[1][...], small_held[2][...], lax.axis_index(GROUP_AXES), group_count
            )
            boundary_held[...] = jnp.broadcast_to(boundary, boundary_held.shape)
            boundary_copy.start()
        for step in range(steps):
            block = slice(step * PACK_STEP, (step + 1) * PACK_STEP)
            large_copy(n, step).wait()
            array = large_held[n, block]
            if n < 2:
                widened = array.astype(jnp.float32)
                inverse = lax.rsqrt(jnp.mean(widened * widened, axis=-1, keepdims=True) + epsilon)
                array = (widened * inverse * small_held[3 + n][...]).astype(jnp.bfloat16)
            if n == 3:
                position = (
                    lax.axis_index("blk") * rows + step * PACK_STEP
                    + lax.broadcasted_iota(jnp.int32, (PACK_STEP, 1), 0)
                )
                row_weight = jnp.where(position < boundary, weight_first, weight_last)
                array = (array.astype(jnp.float32) * row_weight).astype(jnp.bfloat16)
            if n == 2:
                continue
            for d in range(cycle):
                for h in range(heads):
                    start = (d * heads + h) * HEAD_DIM
                    packed_held[d, h, n, block] = array[:, start : start + HEAD_DIM]
        for copy in out_copies(n):
            copy.start()
    for n in order:
        for copy in out_copies(n):
            copy.wait()
    boundary_copy.wait()


def pack(q_raw, k_raw, values, grad_out, q_gain, k_gain, counts, assignment, loader, cycle, group_count):
    rows, width = q_raw.shape
    packed = jax.ShapeDtypeStruct((cycle, width // cycle // HEAD_DIM, KINDS, rows, HEAD_DIM), jnp.bfloat16)
    small = (counts, assignment, loader, q_gain, k_gain)
    return pl.pallas_call(
        functools.partial(pack_kernel, group_count, cycle),
        in_specs=[pl.BlockSpec(memory_space=pl.ANY)] * 9,
        out_specs=[pl.BlockSpec(memory_space=pl.ANY)] * 2,
        out_shape=[packed, jax.ShapeDtypeStruct((8, 128), jnp.int32)],
        scratch_shapes=[pltpu.VMEM(x.shape, x.dtype) for x in small]
        + [
            pltpu.VMEM((KINDS, rows, width), jnp.bfloat16),
            pltpu.VMEM(packed.shape, packed.dtype),
            pltpu.VMEM((8, 128), jnp.int32),
            pltpu.SemaphoreType.DMA((5,)),
            pltpu.SemaphoreType.DMA((KINDS, rows // PACK_STEP)),
            pltpu.SemaphoreType.DMA((cycle, KINDS + packed.shape[1])),
            pltpu.SemaphoreType.DMA(()),
        ],
        compiler_params=pltpu.CompilerParams(vmem_limit_bytes=60 * MIB),
        cost_estimate=pl.CostEstimate(flops=12 * rows * width, bytes_accessed=16 * rows * width, transcendentals=rows),
        name="pack",
    )(*small, q_raw, k_raw, values, grad_out)


def dot(a, b, a_dim, b_dim):
    return lax.dot_general(a, b, (((a_dim,), (b_dim,)), ((), ())), preferred_element_type=jnp.float32)


def fold(array, op):
    return op(array.reshape(-1, 8, array.shape[-1]), axis=0)


def attention_kernel(cycle, boundary_ref, x_ref, *rest):
    o_refs, part_ref = rest[:cycle], rest[cycle]
    side_ref, score_ref, grad_ref, softmax_ref, weighted_ref, score_grad_ref, held_ref = rest[cycle + 1 :]
    _, _, kinds, rows, width = x_ref.shape
    heads = HEAD_STEP
    slots = cycle * rows
    scale = HEAD_DIM ** (-0.5)
    boundary = boundary_ref[0:1, 0:1]
    step = pl.program_id(0)
    place = lax.axis_index("blk")
    key_steps = [slice(j, j + KEY_STEP) for j in range(0, slots, KEY_STEP)]
    query_side = (lax.broadcasted_iota(jnp.int32, (1, slots), 1) < boundary).astype(jnp.int32)

    @pl.when(step == 0)
    def _():
        side_ref[...] = (lax.broadcasted_iota(jnp.int32, side_ref.shape, 0) < boundary).astype(jnp.int32)
        part_ref[...] = jnp.zeros_like(part_ref)

    def operands(h):
        return [x_ref[:, step * heads + h, a].reshape(slots, width) for a in range(kinds)]

    def products(h):
        q, k, v, g = operands(h)
        scores = dot(k, q, 1, 1)
        top = None
        for down in key_steps:
            side = jnp.concatenate([side_ref[down]] * (slots // 128), axis=1)
            block = jnp.where(side == query_side, scores[down], masked_score)
            score_ref[h, down] = block
            block = fold(block, jnp.max)
            top = block if top is None else jnp.maximum(top, block)
        grad_ref[h] = dot(v, g, 1, 1)
        return jnp.max(top, axis=0, keepdims=True)

    def weights(h, top):
        total = 0.0
        for down in key_steps:
            block = jnp.exp2((score_ref[h, down] - top) * (scale * log2_e))
            score_ref[h, down] = block
            total += fold(block, jnp.sum)
        inverse = 1.0 / jnp.sum(total, axis=0, keepdims=True)
        row_delta = 0.0
        for down in key_steps:
            softmax = score_ref[h, down] * inverse
            weighted = softmax * grad_ref[h, down]
            row_delta += fold(weighted, jnp.sum)
            softmax_ref[h, down] = softmax.astype(jnp.bfloat16)
            weighted_ref[h, down] = weighted.astype(jnp.bfloat16)
        row_delta = jnp.sum(row_delta, axis=0, keepdims=True)
        for down in key_steps:
            softmax = score_ref[h, down] * inverse
            score_grad_ref[h, down] = (softmax * (grad_ref[h, down] - row_delta)).astype(jnp.bfloat16)
        return row_delta

    def results(h, row_delta):
        q, k, v, g = operands(h)
        both = dot(jnp.concatenate([v, k], axis=1), softmax_ref[h], 0, 0)
        query_grad = (scale * (dot(k, weighted_ref[h], 0, 0) - row_delta * both[width:])).T
        key_grad = scale * dot(score_grad_ref[h], q, 1, 0)
        held_ref[h, 0] = both[:width].T.astype(jnp.bfloat16)
        held_ref[h, 1] = query_grad.astype(jnp.bfloat16)
        held_ref[h, 2] = key_grad.astype(jnp.bfloat16)
        held_ref[h, 3] = dot(softmax_ref[h], g, 1, 0).astype(jnp.bfloat16)
        for s in range(cycle):
            first = pl.multiple_of(lax.rem(place + cycle - s, cycle) * rows, rows)
            o_refs[s][step * heads + h] = held_ref[h, :, pl.ds(first, rows), :]
        query_part = jnp.sum(query_grad * q.astype(jnp.float32), axis=0, keepdims=True)
        key_part = jnp.sum(key_grad * k.astype(jnp.float32), axis=0, keepdims=True)
        parts = jnp.concatenate([query_part, key_part], axis=0)
        at = pl.ds(2 * (step * heads + h), 2)
        part_ref[:, at, :] = jnp.broadcast_to(parts, (part_ref.shape[0], 2, width))

    top = products(0)
    for h in range(heads):
        row_delta = weights(h, top)
        if h + 1 < heads:
            top = products(h + 1)
        results(h, row_delta)


def attention(boundary, arrived, copies):
    cycle, heads, kinds, rows, width = arrived.shape
    slots = cycle * rows
    parts = (copies, PART_ROWS, width)
    square = (HEAD_STEP, slots, slots)
    out = pl.pallas_call(
        functools.partial(attention_kernel, cycle),
        grid=(heads // HEAD_STEP,),
        in_specs=[
            pl.BlockSpec(memory_space=pltpu.VMEM),
            pl.BlockSpec(memory_space=pltpu.VMEM),
        ],
        out_specs=[pl.BlockSpec(memory_space=pltpu.VMEM)] * cycle
        + [pl.BlockSpec(parts, lambda h: (0, 0, 0))],
        out_shape=[jax.ShapeDtypeStruct((heads, kinds, rows, width), jnp.bfloat16)] * cycle
        + [jax.ShapeDtypeStruct(parts, jnp.float32)],
        scratch_shapes=[
            pltpu.VMEM((slots, 128), jnp.int32),
            pltpu.VMEM(square, jnp.float32),
            pltpu.VMEM(square, jnp.float32),
            pltpu.VMEM(square, jnp.bfloat16),
            pltpu.VMEM(square, jnp.bfloat16),
            pltpu.VMEM(square, jnp.bfloat16),
            pltpu.VMEM((HEAD_STEP, kinds, slots, width), jnp.bfloat16),
        ],
        compiler_params=pltpu.CompilerParams(vmem_limit_bytes=32 * MIB),
        cost_estimate=pl.CostEstimate(
            flops=14 * heads * slots * slots * width, bytes_accessed=16 * slots * width * heads,
            transcendentals=heads * slots * slots,
        ),
        name="attention",
    )(boundary, arrived)
    return out[:cycle], out[cycle]


def slot_order(cycle):
    return sorted(range(cycle), key=lambda s: -min(s, cycle - s))


def finish_kernel(cycle, *refs):
    back_refs, raws, gains = [None] * cycle, refs[cycle : cycle + 2], refs[cycle + 2 : cycle + 4]
    for s, ref in zip(slot_order(cycle), refs):
        back_refs[s] = ref
    att_ref, dq_ref, dk_ref, dv_ref = refs[cycle + 4 : cycle + 8]
    grad_held, grad_sems, copy_sems = refs[cycle + 8 :]
    heads, kinds, rows, _ = back_refs[0].shape
    share = heads * HEAD_DIM
    width = share * cycle
    steps = rows // ROW_STEP
    place = lax.axis_index("blk")
    starts = [pl.multiple_of(lax.rem(place + s, cycle) * share, share) for s in range(cycle)]

    def grad_copy(n, step):
        block = pl.ds(step * ROW_STEP, ROW_STEP)
        return pltpu.make_async_copy(
            grad_held.at[n, block], (dq_ref, dk_ref)[n].at[block], grad_sems.at[n, step]
        )

    def plain_copy(n, s, h):
        target = (att_ref, dv_ref)[n].at[:, pl.ds(starts[s] + h * HEAD_DIM, HEAD_DIM)]
        return pltpu.make_async_copy(back_refs[s].at[h, 3 * n], target, copy_sems.at[n, s, h])

    plain = [plain_copy(n, s, h) for n in range(2) for s in range(cycle) for h in range(heads)]
    for copy in plain:
        copy.start()
    for step in range(steps):
        block = slice(step * ROW_STEP, (step + 1) * ROW_STEP)
        for n in range(2):
            raw = [raws[n][block, pl.ds(start, share)].astype(jnp.float32) for start in starts]
            grad = [
                jnp.concatenate([back[h, 1 + n, block] for h in range(heads)], axis=1).astype(jnp.float32)
                * gains[n][:, pl.ds(start, share)]
                for back, start in zip(back_refs, starts)
            ]
            square = sum(jnp.sum(x * x, axis=-1, keepdims=True) for x in raw)
            along = sum(jnp.sum(x * y, axis=-1, keepdims=True) for x, y in zip(raw, grad))
            inverse = lax.rsqrt(square / width + epsilon)
            along = along * inverse * inverse / width
            for x, y, start in zip(raw, grad, starts):
                grad_held[n, block, pl.ds(start, share)] = (inverse * (y - x * along)).astype(jnp.bfloat16)
            grad_copy(n, step).start()
    for copy in plain:
        copy.wait()
    for step in range(steps):
        for n in range(2):
            grad_copy(n, step).wait()


def finish(back, q_raw, k_raw, q_gain, k_gain):
    rows, width = q_raw.shape
    cycle = len(back)
    heads = back[0].shape[0]
    steps = rows // ROW_STEP
    return pl.pallas_call(
        functools.partial(finish_kernel, cycle),
        in_specs=[whole_block(back[0].shape)] * cycle + [whole_block((rows, width))] * 2 + [whole_block((1, width))] * 2,
        out_specs=[pl.BlockSpec(memory_space=pl.ANY)] * 4,
        out_shape=[jax.ShapeDtypeStruct((rows, width), jnp.bfloat16)] * 4,
        scratch_shapes=[
            pltpu.VMEM((2, rows, width), jnp.bfloat16),
            pltpu.SemaphoreType.DMA((2, steps)),
            pltpu.SemaphoreType.DMA((2, cycle, heads)),
        ],
        compiler_params=pltpu.CompilerParams(vmem_limit_bytes=32 * MIB),
        cost_estimate=pl.CostEstimate(flops=20 * rows * width, bytes_accessed=20 * rows * width, transcendentals=rows),
        name="finish",
    )(*(back[s] for s in slot_order(cycle)), q_raw, k_raw, q_gain, k_gain)


def respread_kernel(part_ref, o_ref):
    o_ref[...] = jnp.broadcast_to(jnp.sum(part_ref[...], axis=0, keepdims=True), o_ref.shape)


def respread(part, copies):
    out_shape = (copies,) + part.shape[1:]
    return pl.pallas_call(
        respread_kernel,
        in_specs=[whole_block(part.shape)],
        out_specs=whole_block(out_shape),
        out_shape=jax.ShapeDtypeStruct(out_shape, jnp.float32),
        compiler_params=pltpu.CompilerParams(vmem_limit_bytes=32 * MIB),
        name="respread",
    )(part)


def gain_grad_kernel(part_ref, q_gain_ref, k_gain_ref, q_ref, k_ref):
    total = jnp.sum(part_ref[...], axis=0)
    cycle, count, _ = total.shape
    for n, (gain_ref, out_ref) in enumerate(((q_gain_ref, q_ref), (k_gain_ref, k_ref))):
        rows = jnp.concatenate(
            [total[d, 2 * h + n : 2 * h + n + 1] for d in range(cycle) for h in range(count // 2)], axis=0
        )
        out_ref[...] = rows / gain_ref[...]


def gain_grad(part, q_gain, k_gain):
    shape = (q_gain.size // 128, 128)
    out = pl.pallas_call(
        gain_grad_kernel,
        in_specs=[whole_block(part.shape)] + [whole_block(shape)] * 2,
        out_specs=[whole_block(shape)] * 2,
        out_shape=[jax.ShapeDtypeStruct(shape, jnp.float32)] * 2,
        compiler_params=pltpu.CompilerParams(vmem_limit_bytes=32 * MIB),
        name="gain_grad",
    )(part, q_gain.reshape(shape), k_gain.reshape(shape))
    return [x.reshape(-1) for x in out]


def swap(array, axes):
    return lax.all_to_all(array, axes, 0, 0, tiled=True)


def body(q_raw, k_raw, values, grad_out, q_gain, k_gain, patch_counts, assignment, loader_shard):
    width = q_raw.shape[1]
    cycle, outer, inner, cores = (lax.axis_size(name) for name in ("blk", *GROUP_AXES))
    q_gain_row, k_gain_row = q_gain.reshape(1, width), k_gain.reshape(1, width)
    tables = (x.reshape(-1, 128) for x in (patch_counts, assignment, loader_shard))
    packed, boundary = pack(
        q_raw, k_raw, values, grad_out, q_gain_row, k_gain_row, *tables, cycle, outer * inner * cores
    )
    slots, part = attention(boundary, swap(packed, "blk"), inner * cores)
    back = list(slots)
    for s in slot_order(cycle)[:-1]:
        back[s] = lax.ppermute(slots[s], "blk", [(i, (i - s) % cycle) for i in range(cycle)])

    part = respread(swap(part, ("y", "c"))[:, : 2 * slots[0].shape[0]], outer * cycle)
    part = swap(part, ("z", "blk"))
    part = part.reshape(outer, cycle, *part.shape[1:])
    return (*finish(back, q_raw, k_raw, q_gain_row, k_gain_row), *gain_grad(part, q_gain, k_gain))


def solution(mesh):
    groups = mesh.shape["dp"]
    cores = math.gcd(groups, 2)
    inner = math.gcd(groups // cores, 8)
    split = Mesh(
        mesh.devices.reshape(mesh.shape["blk"], groups // cores // inner, inner, cores), ("blk", *GROUP_AXES)
    )
    rows = P((*GROUP_AXES, "blk"), None)
    return jax.shard_map(
        body,
        mesh=split,
        in_specs=(rows,) * 4 + (P(),) * 5,
        out_specs=(rows,) * 4 + (P(),) * 2,
        check_vma=False,
    )
```

```python
import functools
import math

import jax
import jax.numpy as jnp
from jax import lax
from jax.experimental import pallas as pl
from jax.experimental.pallas import tpu as pltpu
from jax.sharding import Mesh, PartitionSpec as P

HEAD_DIM = 128
KINDS = 4
PACK_STEP = 128
ROW_STEP = 128
HEAD_STEP = 4
KEY_STEP = 64
PART_ROWS = 24
GROUP_AXES = ("z", "y", "c")
MIB = 1024 * 1024

epsilon = 1e-06
masked_score = -1e30
log2_e = 1.4426950408889634


def whole_block(shape):
    return pl.BlockSpec(memory_space=pltpu.VMEM)


def sum_all(array):
    return jnp.sum(jnp.sum(array, axis=1, keepdims=True), axis=0, keepdims=True)


def group_table(counts, assignment, loader, group_index, group_count):
    shape = counts.shape
    entries = lax.broadcasted_iota(jnp.int32, shape, 0) * shape[1] + lax.broadcasted_iota(
        jnp.int32, shape, 1
    )
    living = counts > 0
    owned = living & (assignment == group_index)
    total = shape[0] * shape[1]
    first = jnp.where(owned, entries, total)
    first = jnp.min(jnp.min(first, axis=1, keepdims=True), axis=0, keepdims=True)
    last = jnp.where(owned, entries, -1)
    last = jnp.max(jnp.max(last, axis=1, keepdims=True), axis=0, keepdims=True)
    boundary = sum_all(jnp.where(entries == first, counts, 0))
    living_total = sum_all(living.astype(jnp.int32))

    def weight_of(entry):
        shard = sum_all(jnp.where(entries == entry, loader, 0))
        shared = sum_all((living & (loader == shard)).astype(jnp.int32))
        return living_total.astype(jnp.float32) / (group_count * shared).astype(jnp.float32)

    return boundary, weight_of(first), weight_of(last)


def pack_kernel(group_count, cycle, *refs):
    small, large = refs[:5], refs[5:9]
    packed_ref, boundary_ref = refs[9:11]
    small_held = refs[11:16]
    large_held, packed_held, boundary_held, small_sems, large_sems, out_sems, boundary_sem = refs[16:]
    boundary_copy = pltpu.make_async_copy(boundary_held, boundary_ref, boundary_sem)
    rows, width = large[0].shape
    steps = rows // PACK_STEP
    heads = width // cycle // HEAD_DIM
    small_copies = [pltpu.make_async_copy(small[n], small_held[n], small_sems.at[n]) for n in range(5)]
    for copy in small_copies:
        copy.start()

    def large_copy(n, step):
        block = pl.ds(step * PACK_STEP, PACK_STEP)
        return pltpu.make_async_copy(large[n].at[block], large_held.at[n, block], large_sems.at[n, step])

    def out_copies(n):
        if n == 2:
            return [
                pltpu.make_async_copy(
                    large_held.at[2, :, pl.ds((d * heads + h) * HEAD_DIM, HEAD_DIM)],
                    packed_ref.at[d, h, 2],
                    out_sems.at[d, KINDS + h],
                )
                for d in range(cycle)
                for h in range(heads)
            ]
        return [
            pltpu.make_async_copy(packed_held.at[d, :, n], packed_ref.at[d, :, n], out_sems.at[d, n])
            for d in range(cycle)
        ]

    order = (2, 0, 1, 3)
    for n in order:
        for step in range(steps):
            large_copy(n, step).start()
    for n in order:
        if n == 0:
            for copy in small_copies[3:]:
                copy.wait()
        if n == 3:
            for copy in small_copies[:3]:
                copy.wait()
            boundary, weight_first, weight_last = group_table(
                small_held[0][...], small_held[1][...], small_held[2][...], lax.axis_index(GROUP_AXES), group_count
            )
            boundary_held[...] = jnp.broadcast_to(boundary, boundary_held.shape)
            boundary_copy.start()
        for step in range(steps):
            block = slice(step * PACK_STEP, (step + 1) * PACK_STEP)
            large_copy(n, step).wait()
            array = large_held[n, block]
            if n < 2:
                widened = array.astype(jnp.float32)
                inverse = lax.rsqrt(jnp.mean(widened * widened, axis=-1, keepdims=True) + epsilon)
                array = (widened * inverse * small_held[3 + n][...]).astype(jnp.bfloat16)
            if n == 3:
                position = (
                    lax.axis_index("blk") * rows + step * PACK_STEP
                    + lax.broadcasted_iota(jnp.int32, (PACK_STEP, 1), 0)
                )
                row_weight = jnp.where(position < boundary, weight_first, weight_last)
                array = (array.astype(jnp.float32) * row_weight).astype(jnp.bfloat16)
            if n == 2:
                continue
            for d in range(cycle):
                for h in range(heads):
                    start = (d * heads + h) * HEAD_DIM
                    packed_held[d, h, n, block] = array[:, start : start + HEAD_DIM]
        for copy in out_copies(n):
            copy.start()
    for n in order:
        for copy in out_copies(n):
            copy.wait()
    boundary_copy.wait()


def pack(q_raw, k_raw, values, grad_out, q_gain, k_gain, counts, assignment, loader, cycle, group_count):
    rows, width = q_raw.shape
    packed = jax.ShapeDtypeStruct((cycle, width // cycle // HEAD_DIM, KINDS, rows, HEAD_DIM), jnp.bfloat16)
    small = (counts, assignment, loader, q_gain, k_gain)
    return pl.pallas_call(
        functools.partial(pack_kernel, group_count, cycle),
        in_specs=[pl.BlockSpec(memory_space=pl.ANY)] * 9,
        out_specs=[pl.BlockSpec(memory_space=pl.ANY)] * 2,
        out_shape=[packed, jax.ShapeDtypeStruct((8, 128), jnp.int32)],
        scratch_shapes=[pltpu.VMEM(x.shape, x.dtype) for x in small]
        + [
            pltpu.VMEM((KINDS, rows, width), jnp.bfloat16),
            pltpu.VMEM(packed.shape, packed.dtype),
            pltpu.VMEM((8, 128), jnp.int32),
            pltpu.SemaphoreType.DMA((5,)),
            pltpu.SemaphoreType.DMA((KINDS, rows // PACK_STEP)),
            pltpu.SemaphoreType.DMA((cycle, KINDS + packed.shape[1])),
            pltpu.SemaphoreType.DMA(()),
        ],
        compiler_params=pltpu.CompilerParams(vmem_limit_bytes=60 * MIB),
        cost_estimate=pl.CostEstimate(flops=12 * rows * width, bytes_accessed=16 * rows * width, transcendentals=rows),
        name="pack",
    )(*small, q_raw, k_raw, values, grad_out)


def dot(a, b, a_dim, b_dim):
    return lax.dot_general(a, b, (((a_dim,), (b_dim,)), ((), ())), preferred_element_type=jnp.float32)


def fold(array, op):
    return op(array.reshape(-1, 8, array.shape[-1]), axis=0)


def attention_kernel(cycle, boundary_ref, x_ref, *rest):
    o_refs, part_ref = rest[:cycle], rest[cycle]
    side_ref, score_ref, grad_ref, softmax_ref, weighted_ref, score_grad_ref, held_ref = rest[cycle + 1 :]
    _, _, kinds, rows, width = x_ref.shape
    heads = HEAD_STEP
    slots = cycle * rows
    scale = HEAD_DIM ** (-0.5)
    boundary = boundary_ref[0:1, 0:1]
    step = pl.program_id(0)
    place = lax.axis_index("blk")
    key_steps = [slice(j, j + KEY_STEP) for j in range(0, slots, KEY_STEP)]
    query_side = (lax.broadcasted_iota(jnp.int32, (1, slots), 1) < boundary).astype(jnp.int32)

    @pl.when(step == 0)
    def _():
        side_ref[...] = (lax.broadcasted_iota(jnp.int32, side_ref.shape, 0) < boundary).astype(jnp.int32)
        part_ref[...] = jnp.zeros_like(part_ref)

    def operands(h):
        return [x_ref[:, step * heads + h, a].reshape(slots, width) for a in range(kinds)]

    def products(h):
        q, k, v, g = operands(h)
        scores = dot(k, q, 1, 1)
        top = None
        for down in key_steps:
            side = jnp.concatenate([side_ref[down]] * (slots // 128), axis=1)
            block = jnp.where(side == query_side, scores[down], masked_score)
            score_ref[h, down] = block
            block = fold(block, jnp.max)
            top = block if top is None else jnp.maximum(top, block)
        grad_ref[h] = dot(v, g, 1, 1)
        return jnp.max(top, axis=0, keepdims=True)

    def weights(h, top):
        total = 0.0
        for down in key_steps:
            block = jnp.exp2((score_ref[h, down] - top) * (scale * log2_e))
            score_ref[h, down] = block
            total += fold(block, jnp.sum)
        inverse = 1.0 / jnp.sum(total, axis=0, keepdims=True)
        row_delta = 0.0
        for down in key_steps:
            softmax = score_ref[h, down] * inverse
            weighted = softmax * grad_ref[h, down]
            row_delta += fold(weighted, jnp.sum)
            softmax_ref[h, down] = softmax.astype(jnp.bfloat16)
            weighted_ref[h, down] = weighted.astype(jnp.bfloat16)
        row_delta = jnp.sum(row_delta, axis=0, keepdims=True)
        for down in key_steps:
            softmax = score_ref[h, down] * inverse
            score_grad_ref[h, down] = (softmax * (grad_ref[h, down] - row_delta)).astype(jnp.bfloat16)
        return row_delta

    def results(h, row_delta):
        q, k, v, g = operands(h)
        both = dot(jnp.concatenate([v, k], axis=1), softmax_ref[h], 0, 0)
        query_grad = (scale * (dot(k, weighted_ref[h], 0, 0) - row_delta * both[width:])).T
        key_grad = scale * dot(score_grad_ref[h], q, 1, 0)
        held_ref[h, 0] = both[:width].T.astype(jnp.bfloat16)
        held_ref[h, 1] = query_grad.astype(jnp.bfloat16)
        held_ref[h, 2] = key_grad.astype(jnp.bfloat16)
        held_ref[h, 3] = dot(softmax_ref[h], g, 1, 0).astype(jnp.bfloat16)
        for s in range(cycle):
            first = pl.multiple_of(lax.rem(place + cycle - s, cycle) * rows, rows)
            o_refs[s][step * heads + h] = held_ref[h, :, pl.ds(first, rows), :]
        query_part = jnp.sum(query_grad * q.astype(jnp.float32), axis=0, keepdims=True)
        key_part = jnp.sum(key_grad * k.astype(jnp.float32), axis=0, keepdims=True)
        parts = jnp.concatenate([query_part, key_part], axis=0)
        at = pl.ds(2 * (step * heads + h), 2)
        part_ref[:, at, :] = jnp.broadcast_to(parts, (part_ref.shape[0], 2, width))

    top = products(0)
    for h in range(heads):
        row_delta = weights(h, top)
        if h + 1 < heads:
            top = products(h + 1)
        results(h, row_delta)


def attention(boundary, arrived, copies):
    cycle, heads, kinds, rows, width = arrived.shape
    slots = cycle * rows
    parts = (copies, PART_ROWS, width)
    square = (HEAD_STEP, slots, slots)
    out = pl.pallas_call(
        functools.partial(attention_kernel, cycle),
        grid=(heads // HEAD_STEP,),
        in_specs=[
            pl.BlockSpec(memory_space=pltpu.VMEM),
            pl.BlockSpec(memory_space=pltpu.VMEM),
        ],
        out_specs=[pl.BlockSpec(memory_space=pltpu.VMEM)] * cycle
        + [pl.BlockSpec(parts, lambda h: (0, 0, 0))],
        out_shape=[jax.ShapeDtypeStruct((heads, kinds, rows, width), jnp.bfloat16)] * cycle
        + [jax.ShapeDtypeStruct(parts, jnp.float32)],
        scratch_shapes=[
            pltpu.VMEM((slots, 128), jnp.int32),
            pltpu.VMEM(square, jnp.float32),
            pltpu.VMEM(square, jnp.float32),
            pltpu.VMEM(square, jnp.bfloat16),
            pltpu.VMEM(square, jnp.bfloat16),
            pltpu.VMEM(square, jnp.bfloat16),
            pltpu.VMEM((HEAD_STEP, kinds, slots, width), jnp.bfloat16),
        ],
        compiler_params=pltpu.CompilerParams(vmem_limit_bytes=32 * MIB),
        cost_estimate=pl.CostEstimate(
            flops=14 * heads * slots * slots * width, bytes_accessed=16 * slots * width * heads,
            transcendentals=heads * slots * slots,
        ),
        name="attention",
    )(boundary, arrived)
    return out[:cycle], out[cycle]


def slot_order(cycle):
    return sorted(range(cycle), key=lambda s: -min(s, cycle - s))


def finish_kernel(cycle, *refs):
    back_refs, raws, gains = [None] * cycle, refs[cycle : cycle + 2], refs[cycle + 2 : cycle + 4]
    for s, ref in zip(slot_order(cycle), refs):
        back_refs[s] = ref
    att_ref, dq_ref, dk_ref, dv_ref = refs[cycle + 4 : cycle + 8]
    grad_held, grad_sems, copy_sems = refs[cycle + 8 :]
    heads, kinds, rows, _ = back_refs[0].shape
    share = heads * HEAD_DIM
    width = share * cycle
    steps = rows // ROW_STEP
    place = lax.axis_index("blk")
    starts = [pl.multiple_of(lax.rem(place + s, cycle) * share, share) for s in range(cycle)]

    def grad_copy(n, step):
        block = pl.ds(step * ROW_STEP, ROW_STEP)
        return pltpu.make_async_copy(
            grad_held.at[n, block], (dq_ref, dk_ref)[n].at[block], grad_sems.at[n, step]
        )

    def plain_copy(n, s, h):
        target = (att_ref, dv_ref)[n].at[:, pl.ds(starts[s] + h * HEAD_DIM, HEAD_DIM)]
        return pltpu.make_async_copy(back_refs[s].at[h, 3 * n], target, copy_sems.at[n, s, h])

    plain = [plain_copy(n, s, h) for n in range(2) for s in range(cycle) for h in range(heads)]
    for copy in plain:
        copy.start()
    for step in range(steps):
        block = slice(step * ROW_STEP, (step + 1) * ROW_STEP)
        for n in range(2):
            raw = [raws[n][block, pl.ds(start, share)].astype(jnp.float32) for start in starts]
            grad = [
                jnp.concatenate([back[h, 1 + n, block] for h in range(heads)], axis=1).astype(jnp.float32)
                * gains[n][:, pl.ds(start, share)]
                for back, start in zip(back_refs, starts)
            ]
            square = sum(jnp.sum(x * x, axis=-1, keepdims=True) for x in raw)
            along = sum(jnp.sum(x * y, axis=-1, keepdims=True) for x, y in zip(raw, grad))
            inverse = lax.rsqrt(square / width + epsilon)
            along = along * inverse * inverse / width
            for x, y, start in zip(raw, grad, starts):
                grad_held[n, block, pl.ds(start, share)] = (inverse * (y - x * along)).astype(jnp.bfloat16)
            grad_copy(n, step).start()
    for copy in plain:
        copy.wait()
    for step in range(steps):
        for n in range(2):
            grad_copy(n, step).wait()


def finish(back, q_raw, k_raw, q_gain, k_gain):
    rows, width = q_raw.shape
    cycle = len(back)
    heads = back[0].shape[0]
    steps = rows // ROW_STEP
    return pl.pallas_call(
        functools.partial(finish_kernel, cycle),
        in_specs=[whole_block(back[0].shape)] * cycle + [whole_block((rows, width))] * 2 + [whole_block((1, width))] * 2,
        out_specs=[pl.BlockSpec(memory_space=pl.ANY)] * 4,
        out_shape=[jax.ShapeDtypeStruct((rows, width), jnp.bfloat16)] * 4,
        scratch_shapes=[
            pltpu.VMEM((2, rows, width), jnp.bfloat16),
            pltpu.SemaphoreType.DMA((2, steps)),
            pltpu.SemaphoreType.DMA((2, cycle, heads)),
        ],
        compiler_params=pltpu.CompilerParams(vmem_limit_bytes=32 * MIB),
        cost_estimate=pl.CostEstimate(flops=20 * rows * width, bytes_accessed=20 * rows * width, transcendentals=rows),
        name="finish",
    )(*(back[s] for s in slot_order(cycle)), q_raw, k_raw, q_gain, k_gain)


def respread_kernel(part_ref, o_ref):
    total = jnp.sum(part_ref[:, : o_ref.shape[1]], axis=0, keepdims=True)
    o_ref[...] = jnp.broadcast_to(total, o_ref.shape)


def respread(part, rows, copies):
    out_shape = (copies, rows, part.shape[2])
    return pl.pallas_call(
        respread_kernel,
        in_specs=[whole_block(part.shape)],
        out_specs=whole_block(out_shape),
        out_shape=jax.ShapeDtypeStruct(out_shape, jnp.float32),
        compiler_params=pltpu.CompilerParams(vmem_limit_bytes=32 * MIB),
        name="respread",
    )(part)


def gain_grad_kernel(part_ref, q_gain_ref, k_gain_ref, q_ref, k_ref):
    total = jnp.sum(part_ref[...], axis=0)
    cycle, count, _ = total.shape
    for n, (gain_ref, out_ref) in enumerate(((q_gain_ref, q_ref), (k_gain_ref, k_ref))):
        rows = jnp.concatenate(
            [total[d, 2 * h + n : 2 * h + n + 1] for d in range(cycle) for h in range(count // 2)], axis=0
        )
        out_ref[...] = rows / gain_ref[...]


def gain_grad(part, q_gain, k_gain):
    shape = (q_gain.size // 128, 128)
    out = pl.pallas_call(
        gain_grad_kernel,
        in_specs=[whole_block(part.shape)] + [whole_block(shape)] * 2,
        out_specs=[whole_block(shape)] * 2,
        out_shape=[jax.ShapeDtypeStruct(shape, jnp.float32)] * 2,
        compiler_params=pltpu.CompilerParams(vmem_limit_bytes=32 * MIB),
        name="gain_grad",
    )(part, q_gain.reshape(shape), k_gain.reshape(shape))
    return [x.reshape(-1) for x in out]


def swap(array, axes):
    return lax.all_to_all(array, axes, 0, 0, tiled=True)


def body(q_raw, k_raw, values, grad_out, q_gain, k_gain, patch_counts, assignment, loader_shard):
    width = q_raw.shape[1]
    cycle, outer, inner, cores = (lax.axis_size(name) for name in ("blk", *GROUP_AXES))
    q_gain_row, k_gain_row = q_gain.reshape(1, width), k_gain.reshape(1, width)
    tables = (x.reshape(-1, 128) for x in (patch_counts, assignment, loader_shard))
    packed, boundary = pack(
        q_raw, k_raw, values, grad_out, q_gain_row, k_gain_row, *tables, cycle, outer * inner * cores
    )
    slots, part = attention(boundary, swap(packed, "blk"), inner * cores)
    back = list(slots)
    for s in slot_order(cycle)[:-1]:
        back[s] = lax.ppermute(slots[s], "blk", [(i, (i - s) % cycle) for i in range(cycle)])

    part = respread(swap(part, ("y", "c")), 2 * slots[0].shape[0], outer * cycle)
    part = swap(part, ("z", "blk"))
    part = part.reshape(outer, cycle, *part.shape[1:])
    return (*finish(back, q_raw, k_raw, q_gain_row, k_gain_row), *gain_grad(part, q_gain, k_gain))


def solution(mesh):
    groups = mesh.shape["dp"]
    cores = math.gcd(groups, 2)
    inner = math.gcd(groups // cores, 8)
    split = Mesh(
        mesh.devices.reshape(mesh.shape["blk"], groups // cores // inner, inner, cores), ("blk", *GROUP_AXES)
    )
    rows = P((*GROUP_AXES, "blk"), None)
    return jax.shard_map(
        body,
        mesh=split,
        in_specs=(rows,) * 4 + (P(),) * 5,
        out_specs=(rows,) * 4 + (P(),) * 2,
        check_vma=False,
    )
```

```python
import functools
import math

import jax
import jax.numpy as jnp
from jax import lax
from jax.experimental import pallas as pl
from jax.experimental.pallas import tpu as pltpu
from jax.sharding import Mesh, PartitionSpec as P

HEAD_DIM = 128
KINDS = 4
PACK_STEP = 128
ROW_STEP = 128
KEY_STEP = 64
PART_ROWS = 24
GROUP_AXES = ("z", "y", "c")
MIB = 1024 * 1024

epsilon = 1e-06
masked_score = -1e30
log2_e = 1.4426950408889634


def whole_block(shape):
    return pl.BlockSpec(memory_space=pltpu.VMEM)


def sum_all(array):
    return jnp.sum(jnp.sum(array, axis=1, keepdims=True), axis=0, keepdims=True)


def group_table(counts, assignment, loader, group_index, group_count):
    shape = counts.shape
    entries = lax.broadcasted_iota(jnp.int32, shape, 0) * shape[1] + lax.broadcasted_iota(
        jnp.int32, shape, 1
    )
    living = counts > 0
    owned = living & (assignment == group_index)
    total = shape[0] * shape[1]
    first = jnp.where(owned, entries, total)
    first = jnp.min(jnp.min(first, axis=1, keepdims=True), axis=0, keepdims=True)
    last = jnp.where(owned, entries, -1)
    last = jnp.max(jnp.max(last, axis=1, keepdims=True), axis=0, keepdims=True)
    boundary = sum_all(jnp.where(entries == first, counts, 0))
    living_total = sum_all(living.astype(jnp.int32))

    def weight_of(entry):
        shard = sum_all(jnp.where(entries == entry, loader, 0))
        shared = sum_all((living & (loader == shard)).astype(jnp.int32))
        return living_total.astype(jnp.float32) / (group_count * shared).astype(jnp.float32)

    return boundary, weight_of(first), weight_of(last)


def pack_kernel(group_count, cycle, *refs):
    small, large = refs[:5], refs[5:9]
    packed_ref, boundary_ref = refs[9:11]
    small_held = refs[11:16]
    large_held, packed_held, boundary_held, small_sems, large_sems, out_sems, boundary_sem = refs[16:]
    boundary_copy = pltpu.make_async_copy(boundary_held, boundary_ref, boundary_sem)
    rows, width = large[0].shape
    steps = rows // PACK_STEP
    heads = width // cycle // HEAD_DIM
    small_copies = [pltpu.make_async_copy(small[n], small_held[n], small_sems.at[n]) for n in range(5)]
    for copy in small_copies:
        copy.start()

    def large_copy(n, step):
        block = pl.ds(step * PACK_STEP, PACK_STEP)
        return pltpu.make_async_copy(large[n].at[block], large_held.at[n, block], large_sems.at[n, step])

    def out_copies(n):
        if n == 2:
            return [
                pltpu.make_async_copy(
                    large_held.at[2, :, pl.ds((d * heads + h) * HEAD_DIM, HEAD_DIM)],
                    packed_ref.at[d, h, 2],
                    out_sems.at[d, KINDS + h],
                )
                for d in range(cycle)
                for h in range(heads)
            ]
        return [
            pltpu.make_async_copy(packed_held.at[d, :, n], packed_ref.at[d, :, n], out_sems.at[d, n])
            for d in range(cycle)
        ]

    order = (2, 0, 1, 3)
    for n in order:
        for step in range(steps):
            large_copy(n, step).start()
    for n in order:
        if n == 0:
            for copy in small_copies[3:]:
                copy.wait()
        if n == 3:
            for copy in small_copies[:3]:
                copy.wait()
            boundary, weight_first, weight_last = group_table(
                small_held[0][...], small_held[1][...], small_held[2][...], lax.axis_index(GROUP_AXES), group_count
            )
            boundary_held[...] = jnp.broadcast_to(boundary, boundary_held.shape)
            boundary_copy.start()
        for step in range(steps):
            block = slice(step * PACK_STEP, (step + 1) * PACK_STEP)
            large_copy(n, step).wait()
            array = large_held[n, block]
            if n < 2:
                widened = array.astype(jnp.float32)
                inverse = lax.rsqrt(jnp.mean(widened * widened, axis=-1, keepdims=True) + epsilon)
                array = (widened * inverse * small_held[3 + n][...]).astype(jnp.bfloat16)
            if n == 3:
                position = (
                    lax.axis_index("blk") * rows + step * PACK_STEP
                    + lax.broadcasted_iota(jnp.int32, (PACK_STEP, 1), 0)
                )
                row_weight = jnp.where(position < boundary, weight_first, weight_last)
                array = (array.astype(jnp.float32) * row_weight).astype(jnp.bfloat16)
            if n == 2:
                continue
            for d in range(cycle):
                for h in range(heads):
                    start = (d * heads + h) * HEAD_DIM
                    packed_held[d, h, n, block] = array[:, start : start + HEAD_DIM]
        for copy in out_copies(n):
            copy.start()
    for n in order:
        for copy in out_copies(n):
            copy.wait()
    boundary_copy.wait()


def pack(q_raw, k_raw, values, grad_out, q_gain, k_gain, counts, assignment, loader, cycle, group_count):
    rows, width = q_raw.shape
    packed = jax.ShapeDtypeStruct((cycle, width // cycle // HEAD_DIM, KINDS, rows, HEAD_DIM), jnp.bfloat16)
    small = (counts, assignment, loader, q_gain, k_gain)
    return pl.pallas_call(
        functools.partial(pack_kernel, group_count, cycle),
        in_specs=[pl.BlockSpec(memory_space=pl.ANY)] * 9,
        out_specs=[pl.BlockSpec(memory_space=pl.ANY)] * 2,
        out_shape=[packed, jax.ShapeDtypeStruct((8, 128), jnp.int32)],
        scratch_shapes=[pltpu.VMEM(x.shape, x.dtype) for x in small]
        + [
            pltpu.VMEM((KINDS, rows, width), jnp.bfloat16),
            pltpu.VMEM(packed.shape, packed.dtype),
            pltpu.VMEM((8, 128), jnp.int32),
            pltpu.SemaphoreType.DMA((5,)),
            pltpu.SemaphoreType.DMA((KINDS, rows // PACK_STEP)),
            pltpu.SemaphoreType.DMA((cycle, KINDS + packed.shape[1])),
            pltpu.SemaphoreType.DMA(()),
        ],
        compiler_params=pltpu.CompilerParams(vmem_limit_bytes=60 * MIB),
        cost_estimate=pl.CostEstimate(flops=12 * rows * width, bytes_accessed=16 * rows * width, transcendentals=rows),
        name="pack",
    )(*small, q_raw, k_raw, values, grad_out)


def dot(a, b, a_dim, b_dim):
    return lax.dot_general(a, b, (((a_dim,), (b_dim,)), ((), ())), preferred_element_type=jnp.float32)


def fold(array, op):
    return op(array.reshape(-1, 8, array.shape[-1]), axis=0)


def attention_kernel(cycle, boundary_ref, x_ref, *rest):
    o_refs, part_ref = rest[:cycle], rest[cycle]
    side_ref, score_ref, grad_ref, softmax_ref, weighted_ref, score_grad_ref, held_ref = rest[cycle + 1 :]
    _, heads, kinds, rows, width = x_ref.shape
    slots = cycle * rows
    scale = HEAD_DIM ** (-0.5)
    boundary = boundary_ref[0:1, 0:1]
    place = lax.axis_index("blk")
    key_steps = [slice(j, j + KEY_STEP) for j in range(0, slots, KEY_STEP)]
    query_side = (lax.broadcasted_iota(jnp.int32, (1, slots), 1) < boundary).astype(jnp.int32)

    side_ref[...] = (lax.broadcasted_iota(jnp.int32, side_ref.shape, 0) < boundary).astype(jnp.int32)
    part_ref[...] = jnp.zeros_like(part_ref)

    def operands(h):
        return [x_ref[:, h, a].reshape(slots, width) for a in range(kinds)]

    def products(h):
        q, k, v, g = operands(h)
        scores = dot(k, q, 1, 1)
        top = None
        for down in key_steps:
            side = jnp.concatenate([side_ref[down]] * (slots // 128), axis=1)
            block = jnp.where(side == query_side, scores[down], masked_score)
            score_ref[h, down] = block
            block = fold(block, jnp.max)
            top = block if top is None else jnp.maximum(top, block)
        grad_ref[h] = dot(v, g, 1, 1)
        return jnp.max(top, axis=0, keepdims=True)

    def weights(h, top):
        total = 0.0
        for down in key_steps:
            block = jnp.exp2((score_ref[h, down] - top) * (scale * log2_e))
            score_ref[h, down] = block
            total += fold(block, jnp.sum)
        inverse = 1.0 / jnp.sum(total, axis=0, keepdims=True)
        row_delta = 0.0
        for down in key_steps:
            softmax = score_ref[h, down] * inverse
            weighted = softmax * grad_ref[h, down]
            row_delta += fold(weighted, jnp.sum)
            softmax_ref[h, down] = softmax.astype(jnp.bfloat16)
            weighted_ref[h, down] = weighted.astype(jnp.bfloat16)
        row_delta = jnp.sum(row_delta, axis=0, keepdims=True)
        for down in key_steps:
            softmax = score_ref[h, down] * inverse
            score_grad_ref[h, down] = (softmax * (grad_ref[h, down] - row_delta)).astype(jnp.bfloat16)
        return row_delta

    def results(h, row_delta):
        q, k, v, g = operands(h)
        both = dot(jnp.concatenate([v, k], axis=1), softmax_ref[h], 0, 0)
        query_grad = (scale * (dot(k, weighted_ref[h], 0, 0) - row_delta * both[width:])).T
        key_grad = scale * dot(score_grad_ref[h], q, 1, 0)
        held_ref[h, 0] = both[:width].T.astype(jnp.bfloat16)
        held_ref[h, 1] = query_grad.astype(jnp.bfloat16)
        held_ref[h, 2] = key_grad.astype(jnp.bfloat16)
        held_ref[h, 3] = dot(softmax_ref[h], g, 1, 0).astype(jnp.bfloat16)
        for s in range(cycle):
            first = pl.multiple_of(lax.rem(place + cycle - s, cycle) * rows, rows)
            o_refs[s][h] = held_ref[h, :, pl.ds(first, rows), :]
        query_part = jnp.sum(query_grad * q.astype(jnp.float32), axis=0, keepdims=True)
        key_part = jnp.sum(key_grad * k.astype(jnp.float32), axis=0, keepdims=True)
        parts = jnp.concatenate([query_part, key_part], axis=0)
        at = slice(2 * h, 2 * h + 2)
        part_ref[:, at, :] = jnp.broadcast_to(parts, (part_ref.shape[0], 2, width))

    top = products(0)
    for h in range(heads):
        row_delta = weights(h, top)
        if h + 1 < heads:
            top = products(h + 1)
        results(h, row_delta)


def attention(boundary, arrived, copies):
    cycle, heads, kinds, rows, width = arrived.shape
    slots = cycle * rows
    parts = (copies, PART_ROWS, width)
    square = (heads, slots, slots)
    out = pl.pallas_call(
        functools.partial(attention_kernel, cycle),
        in_specs=[
            pl.BlockSpec(memory_space=pltpu.VMEM),
            pl.BlockSpec(memory_space=pltpu.VMEM),
        ],
        out_specs=[pl.BlockSpec(memory_space=pltpu.VMEM)] * cycle
        + [pl.BlockSpec(memory_space=pltpu.VMEM)],
        out_shape=[jax.ShapeDtypeStruct((heads, kinds, rows, width), jnp.bfloat16)] * cycle
        + [jax.ShapeDtypeStruct(parts, jnp.float32)],
        scratch_shapes=[
            pltpu.VMEM((slots, 128), jnp.int32),
            pltpu.VMEM(square, jnp.float32),
            pltpu.VMEM(square, jnp.float32),
            pltpu.VMEM(square, jnp.bfloat16),
            pltpu.VMEM(square, jnp.bfloat16),
            pltpu.VMEM(square, jnp.bfloat16),
            pltpu.VMEM((heads, kinds, slots, width), jnp.bfloat16),
        ],
        compiler_params=pltpu.CompilerParams(vmem_limit_bytes=32 * MIB),
        cost_estimate=pl.CostEstimate(
            flops=14 * heads * slots * slots * width, bytes_accessed=16 * slots * width * heads,
            transcendentals=heads * slots * slots,
        ),
        name="attention",
    )(boundary, arrived)
    return out[:cycle], out[cycle]


def slot_order(cycle):
    return sorted(range(cycle), key=lambda s: -min(s, cycle - s))


def finish_kernel(cycle, *refs):
    back_refs, raws, gains = [None] * cycle, refs[cycle : cycle + 2], refs[cycle + 2 : cycle + 4]
    for s, ref in zip(slot_order(cycle), refs):
        back_refs[s] = ref
    att_ref, dq_ref, dk_ref, dv_ref = refs[cycle + 4 : cycle + 8]
    grad_held, grad_sems, copy_sems = refs[cycle + 8 :]
    heads, kinds, rows, _ = back_refs[0].shape
    share = heads * HEAD_DIM
    width = share * cycle
    steps = rows // ROW_STEP
    place = lax.axis_index("blk")
    starts = [pl.multiple_of(lax.rem(place + s, cycle) * share, share) for s in range(cycle)]

    def grad_copy(n, step):
        block = pl.ds(step * ROW_STEP, ROW_STEP)
        return pltpu.make_async_copy(
            grad_held.at[n, block], (dq_ref, dk_ref)[n].at[block], grad_sems.at[n, step]
        )

    def plain_copy(n, s, h):
        target = (att_ref, dv_ref)[n].at[:, pl.ds(starts[s] + h * HEAD_DIM, HEAD_DIM)]
        return pltpu.make_async_copy(back_refs[s].at[h, 3 * n], target, copy_sems.at[n, s, h])

    plain = [plain_copy(n, s, h) for n in range(2) for s in range(cycle) for h in range(heads)]
    for copy in plain:
        copy.start()
    for step in range(steps):
        block = slice(step * ROW_STEP, (step + 1) * ROW_STEP)
        for n in range(2):
            raw = [raws[n][block, pl.ds(start, share)].astype(jnp.float32) for start in starts]
            grad = [
                jnp.concatenate([back[h, 1 + n, block] for h in range(heads)], axis=1).astype(jnp.float32)
                * gains[n][:, pl.ds(start, share)]
                for back, start in zip(back_refs, starts)
            ]
            square = sum(jnp.sum(x * x, axis=-1, keepdims=True) for x in raw)
            along = sum(jnp.sum(x * y, axis=-1, keepdims=True) for x, y in zip(raw, grad))
            inverse = lax.rsqrt(square / width + epsilon)
            along = along * inverse * inverse / width
            for x, y, start in zip(raw, grad, starts):
                grad_held[n, block, pl.ds(start, share)] = (inverse * (y - x * along)).astype(jnp.bfloat16)
            grad_copy(n, step).start()
    for copy in plain:
        copy.wait()
    for step in range(steps):
        for n in range(2):
            grad_copy(n, step).wait()


def finish(back, q_raw, k_raw, q_gain, k_gain):
    rows, width = q_raw.shape
    cycle = len(back)
    heads = back[0].shape[0]
    steps = rows // ROW_STEP
    return pl.pallas_call(
        functools.partial(finish_kernel, cycle),
        in_specs=[whole_block(back[0].shape)] * cycle + [whole_block((rows, width))] * 2 + [whole_block((1, width))] * 2,
        out_specs=[pl.BlockSpec(memory_space=pl.ANY)] * 4,
        out_shape=[jax.ShapeDtypeStruct((rows, width), jnp.bfloat16)] * 4,
        scratch_shapes=[
            pltpu.VMEM((2, rows, width), jnp.bfloat16),
            pltpu.SemaphoreType.DMA((2, steps)),
            pltpu.SemaphoreType.DMA((2, cycle, heads)),
        ],
        compiler_params=pltpu.CompilerParams(vmem_limit_bytes=32 * MIB),
        cost_estimate=pl.CostEstimate(flops=20 * rows * width, bytes_accessed=20 * rows * width, transcendentals=rows),
        name="finish",
    )(*(back[s] for s in slot_order(cycle)), q_raw, k_raw, q_gain, k_gain)


def respread_kernel(part_ref, o_ref):
    total = jnp.sum(part_ref[:, : o_ref.shape[1]], axis=0, keepdims=True)
    o_ref[...] = jnp.broadcast_to(total, o_ref.shape)


def respread(part, rows, copies):
    out_shape = (copies, rows, part.shape[2])
    return pl.pallas_call(
        respread_kernel,
        in_specs=[whole_block(part.shape)],
        out_specs=whole_block(out_shape),
        out_shape=jax.ShapeDtypeStruct(out_shape, jnp.float32),
        compiler_params=pltpu.CompilerParams(vmem_limit_bytes=32 * MIB),
        name="respread",
    )(part)


def gain_grad_kernel(part_ref, q_gain_ref, k_gain_ref, q_ref, k_ref):
    total = jnp.sum(part_ref[...], axis=0)
    cycle, count, _ = total.shape
    for n, (gain_ref, out_ref) in enumerate(((q_gain_ref, q_ref), (k_gain_ref, k_ref))):
        rows = jnp.concatenate(
            [total[d, 2 * h + n : 2 * h + n + 1] for d in range(cycle) for h in range(count // 2)], axis=0
        )
        out_ref[...] = rows / gain_ref[...]


def gain_grad(part, q_gain, k_gain):
    shape = (q_gain.size // 128, 128)
    out = pl.pallas_call(
        gain_grad_kernel,
        in_specs=[whole_block(part.shape)] + [whole_block(shape)] * 2,
        out_specs=[whole_block(shape)] * 2,
        out_shape=[jax.ShapeDtypeStruct(shape, jnp.float32)] * 2,
        compiler_params=pltpu.CompilerParams(vmem_limit_bytes=32 * MIB),
        name="gain_grad",
    )(part, q_gain.reshape(shape), k_gain.reshape(shape))
    return [x.reshape(-1) for x in out]


def swap(array, axes):
    return lax.all_to_all(array, axes, 0, 0, tiled=True)


def body(q_raw, k_raw, values, grad_out, q_gain, k_gain, patch_counts, assignment, loader_shard):
    width = q_raw.shape[1]
    cycle, outer, inner, cores = (lax.axis_size(name) for name in ("blk", *GROUP_AXES))
    q_gain_row, k_gain_row = q_gain.reshape(1, width), k_gain.reshape(1, width)
    tables = (x.reshape(-1, 128) for x in (patch_counts, assignment, loader_shard))
    packed, boundary = pack(
        q_raw, k_raw, values, grad_out, q_gain_row, k_gain_row, *tables, cycle, outer * inner * cores
    )
    slots, part = attention(boundary, swap(packed, "blk"), inner * cores)
    back = list(slots)
    for s in slot_order(cycle)[:-1]:
        back[s] = lax.ppermute(slots[s], "blk", [(i, (i - s) % cycle) for i in range(cycle)])

    part = respread(swap(part, ("y", "c")), 2 * slots[0].shape[0], outer * cycle)
    part = swap(part, ("z", "blk"))
    part = part.reshape(outer, cycle, *part.shape[1:])
    return (*finish(back, q_raw, k_raw, q_gain_row, k_gain_row), *gain_grad(part, q_gain, k_gain))


def solution(mesh):
    groups = mesh.shape["dp"]
    cores = math.gcd(groups, 2)
    inner = math.gcd(groups // cores, 8)
    split = Mesh(
        mesh.devices.reshape(mesh.shape["blk"], groups // cores // inner, inner, cores), ("blk", *GROUP_AXES)
    )
    rows = P((*GROUP_AXES, "blk"), None)
    return jax.shard_map(
        body,
        mesh=split,
        in_specs=(rows,) * 4 + (P(),) * 5,
        out_specs=(rows,) * 4 + (P(),) * 2,
        check_vma=False,
    )
```
